32 devices in a mesh: groups: 2 (over x), seq: 16 (over z, y, core).
Axes of the slice: x: 2, y: 2, z: 4, core: 2. Of those that a mesh axis runs over, the one named last changes fastest.
Arguments:
- dec_query: bfloat16 [512, 4096], P(('groups', 'seq')), parts along dimension 0, may hold values from -55 to 55
- ctx_grad: bfloat16 [512, 4096], P(('groups', 'seq')), parts along dimension 0, may hold values from -6 to 6
- dec_segments: int32 [512], P(('groups', 'seq')), parts along dimension 0, may hold values from 0 to 255
- enc_kv: bfloat16 [4096, 2, 4096], P(('groups', 'seq')), parts along dimension 0, may hold values from -6 to 6
- enc_segments: int32 [4096], P(('groups', 'seq')), parts along dimension 0, may hold values from 0 to 255, as said below
- moe_input: bfloat16 [512, 4096], P(('groups', 'seq')), parts along dimension 0, may hold values from -6 to 6
- moe_grad: bfloat16 [512, 4096], P(('groups', 'seq')), parts along dimension 0, may hold values from -6 to 6
- gate_prob: bfloat16 [512], P(('groups', 'seq')), parts along dimension 0, may hold values from 0.19921875 to 1
- expert_ids: int32 [512], P(('groups', 'seq')), parts along dimension 0, may hold values from 0 to 1
- keep_mask: int32 [512], P(('groups', 'seq')), parts along dimension 0, may hold values from 0 to 1
- w_input: bfloat16 [4096, 16384], P(None, 'seq'), may hold values from -0.09375 to 0.09375
- w_output: bfloat16 [16384, 4096], P('seq'), may hold values from -0.0625 to 0.0625
Outputs:
- query_grad: bfloat16 [512, 4096], P(('groups', 'seq')), parts along dimension 0
- kv_grad: bfloat16 [4096, 2, 4096], P(('groups', 'seq')), parts along dimension 0
- moe_input_grad: bfloat16 [512, 4096], P(('groups', 'seq')), parts along dimension 0
- gate_grad: float32 [512], P(('groups', 'seq')), parts along dimension 0
- w_input_grad: bfloat16 [8192, 16384], P('groups', 'seq'), parts along dimension 0
- w_output_grad: bfloat16 [16384, 8192], P('seq', 'groups'), parts along dimension 1
The draws below stay inside these ranges and needn't reach their ends.
There are 2 independent parts, one for each index of `groups`. The reference program is written for one: setup_inputs(seed, part) draws one part's arguments, and reference() takes and returns one part's arrays. A program takes and returns all parts, laid end to end along the dimension named above; an argument that names none is the same for every part. Nothing has to cross between parts.
Inputs may be any that keep to these rules, and one draw needn't show every extreme that they name: `enc_segments`: segment ids never fall along the rows; the encoder rows of a decoder token's document lie within 64 rows beyond the encoder rows of the token's device on either side, and every decoder token's document has two or more encoder rows.
All inputs are finite; a program needn't handle non-finite values.
Results may differ from the reference program's by a relative error of at most 0.0091.
Values may be sent and summed in bfloat16 or wider, within the bound.
No kernel may reach another device: no remote copies, remote signals or barrier semaphores. Data moves between devices by JAX's collectives and lax.ppermute only.
A program may use at most 192 MiB of HBM per device.

```python
import jax
import jax.numpy as jnp
from jax import lax

D = 4096
HEADS = 32
HEAD_DIM = 128
FF = 8192
EXPERTS = 2
RATIO = 8
TOK_DEV = 16
CAP = 10
DEC = 256
ENC = 2048
HD = 4096


def shared_base(key):
    key = jax.random.fold_in(key, 101)
    return jnp.clip(jax.random.normal(key, (ENC, HEADS * HEAD_DIM), jnp.float32), -6.0, 6.0)


def segment_layout(key):
    key = jax.random.fold_in(key, 202)
    first, second = jax.random.split(key)
    rows = jnp.arange(DEC)
    forced = rows % TOK_DEV == TOK_DEV // 2
    quiet = (rows > TOK_DEV // 2) & (rows < TOK_DEV // 2 + TOK_DEV)
    flags = (jax.random.randint(first, (DEC,), 0, 6) == 0) & jnp.logical_not(quiet)
    flags = flags | forced | (rows == 0)
    jitter = jax.random.randint(second, (DEC,), -1, 2)
    jitter = jnp.where(forced | (rows == 0), 0, jitter)
    flag_ints = flags.astype(jnp.int32)
    offset = DEC - jnp.sum(flag_ints)
    dec_doc = jnp.cumsum(flag_ints) - 1 + offset
    starts = RATIO * rows + jitter
    enc_flags = jnp.zeros((ENC,), jnp.int32).at[starts].max(flag_ints)
    enc_doc = jnp.cumsum(enc_flags) - 1 + offset
    return (dec_doc.astype(jnp.int32), enc_doc.astype(jnp.int32))


def route_layout(key):
    key = jax.random.fold_in(key, 303)
    first, second, third, fourth = jax.random.split(key, 4)
    blocks = DEC // TOK_DEV
    favoured = jax.random.randint(first, (), 0, EXPERTS)
    noise = jax.random.randint(second, (blocks, TOK_DEV), 0, 1 << 20) * TOK_DEV + jnp.arange(TOK_DEV)[None, :]
    ranking = jnp.argsort(jnp.argsort(noise, axis=1), axis=1)
    forced = ranking < CAP
    choices = jnp.where(forced, favoured, jax.random.randint(third, (blocks, TOK_DEV), 0, EXPERTS))
    kept = jnp.where(forced, 1, (jax.random.randint(fourth, (blocks, TOK_DEV), 0, 4) > 0).astype(jnp.int32))
    return (choices.reshape(DEC).astype(jnp.int32), kept.reshape(DEC).astype(jnp.int32))


def draw_dec_query(key, part):
    key = jax.random.fold_in(key, 7)
    drawn = jnp.clip(jax.random.normal(key, (DEC, HEADS * HEAD_DIM), jnp.float32), -6.0, 6.0)
    return drawn.astype(jnp.bfloat16)


def draw_enc_kv(key, part):
    base = shared_base(key)
    key = jax.random.fold_in(key, 13)
    values = jnp.clip(jax.random.normal(key, (ENC, HEADS * HEAD_DIM), jnp.float32), -6.0, 6.0)
    return jnp.stack([base, values], axis=1).astype(jnp.bfloat16)


def draw_dec_segments(key, part):
    dec_doc, enc_doc = segment_layout(key)
    return dec_doc


def draw_enc_segments(key, part):
    dec_doc, enc_doc = segment_layout(key)
    return enc_doc


def draw_expert_ids(key, part):
    choices, kept = route_layout(key)
    return choices


def draw_keep_mask(key, part):
    choices, kept = route_layout(key)
    return kept


def shard_levels(key, extent, pieces, low, top_value):
    def one(axis_at, shards_of):
        draws = jax.random.uniform(jax.random.fold_in(jax.random.fold_in(key, 6), axis_at), (shards_of,), jnp.float32, low / len(pieces), top_value / len(pieces))
        return jnp.repeat(jnp.exp(draws), extent[axis_at] // shards_of).reshape((-1,) + (1,) * (len(extent) - axis_at - 1))

    factor_of = one(*pieces[0])
    for cut in pieces[1:]:
        factor_of = factor_of * one(*cut)
    return factor_of


def bell_draw(own_key, shape, scale, most, cuts=(), kind=jnp.bfloat16):
    entries = jax.random.normal(own_key, shape, jnp.float32) * scale
    if len(cuts) > 0:
        entries = shard_levels(own_key, shape, cuts, -0.22, 0.18) * entries
    return jnp.clip(entries, min=-most, max=most).astype(kind)


def setup_inputs(seed: int = 0, part: int = 0) -> dict:
    arg_keys = jax.random.split(jax.random.key(seed), 13)
    part_keys = jax.random.split(jax.random.fold_in(arg_keys[12], part), 13)
    dec_query = draw_dec_query(jax.random.fold_in(jax.random.fold_in(arg_keys[12], part), 71), part)
    ctx_grad = bell_draw(part_keys[1], (DEC, HD), 1.0, 6.0, ((0, 16),))
    dec_segments = draw_dec_segments(jax.random.fold_in(jax.random.fold_in(arg_keys[12], part), 71), part)
    enc_kv = draw_enc_kv(jax.random.fold_in(jax.random.fold_in(arg_keys[12], part), 71), part)
    enc_segments = draw_enc_segments(jax.random.fold_in(jax.random.fold_in(arg_keys[12], part), 71), part)
    moe_input = bell_draw(part_keys[5], (DEC, D), 1.0, 6.0, ((0, 16),))
    moe_grad = bell_draw(part_keys[6], (DEC, D), 1.0, 6.0, ((0, 16),))
    gate_prob = jnp.clip(0.19921875 + 0.80078125 * jax.random.uniform(part_keys[7], (DEC,), jnp.float32) ** shard_levels(part_keys[7], (DEC,), ((0, 16),), -0.2, 0.2), 0.19921875, 1.0).astype(jnp.bfloat16)
    expert_ids = draw_expert_ids(jax.random.fold_in(jax.random.fold_in(arg_keys[12], part), 71), part)
    keep_mask = draw_keep_mask(jax.random.fold_in(jax.random.fold_in(arg_keys[12], part), 71), part)
    w_input = bell_draw(arg_keys[10], (D, EXPERTS * FF), D ** -0.5, 0.09375, ((1, 16),))
    w_output = bell_draw(arg_keys[11], (EXPERTS * FF, D), FF ** -0.5, 0.0625, ((0, 16),))
    return dict(dec_query=dec_query, ctx_grad=ctx_grad, dec_segments=dec_segments, enc_kv=enc_kv, enc_segments=enc_segments, moe_input=moe_input, moe_grad=moe_grad, gate_prob=gate_prob, expert_ids=expert_ids, keep_mask=keep_mask, w_input=w_input, w_output=w_output)


SCALE = 0.125


def reference(dec_query, ctx_grad, dec_segments, enc_kv, enc_segments, moe_input, moe_grad, gate_prob, expert_ids, keep_mask, w_input, w_output):
    width = HEADS * HEAD_DIM
    keys_wide = enc_kv[:, 0].reshape(ENC, HEADS, HEAD_DIM).astype(jnp.float32)
    values_wide = enc_kv[:, 1].reshape(ENC, HEADS, HEAD_DIM).astype(jnp.float32)
    blocks = DEC // TOK_DEV

    def block_step(carry, items):
        key_acc, value_acc = carry
        block_query, block_upstream, block_segments = items
        queries = block_query.reshape(TOK_DEV, HEADS, HEAD_DIM).astype(jnp.float32)
        upstream = block_upstream.reshape(TOK_DEV, HEADS, HEAD_DIM).astype(jnp.float32)
        allowed = block_segments[:, None] == enc_segments[None, :]
        scores = SCALE * jnp.einsum("qhd,khd->hqk", queries, keys_wide)
        scores = jnp.where(allowed[None], scores, -1e30)
        row_peak = jnp.max(scores, axis=2, keepdims=True)
        exp_scores = jnp.exp(scores - row_peak)
        attn_probs = exp_scores / jnp.sum(exp_scores, axis=2, keepdims=True)
        probs_low = lax.optimization_barrier(attn_probs.astype(jnp.bfloat16))
        probs_wide = probs_low.astype(jnp.float32)
        context = jnp.einsum("hqk,khd->qhd", probs_wide, values_wide)
        row_delta = jnp.sum(upstream * context, axis=2)
        prob_grad = jnp.einsum("qhd,khd->hqk", upstream, values_wide)
        score_grad = lax.optimization_barrier((attn_probs * (prob_grad - row_delta.T[:, :, None])).astype(jnp.bfloat16))
        score_wide = score_grad.astype(jnp.float32)
        block_grad = (SCALE * jnp.einsum("hqk,khd->qhd", score_wide, keys_wide)).astype(jnp.bfloat16).reshape(TOK_DEV, width)
        key_acc = key_acc + SCALE * jnp.einsum("hqk,qhd->khd", score_wide, queries)
        value_acc = value_acc + jnp.einsum("hqk,qhd->khd", probs_wide, upstream)
        return (key_acc, value_acc), block_grad

    start = (jnp.zeros((ENC, HEADS, HEAD_DIM), jnp.float32), jnp.zeros((ENC, HEADS, HEAD_DIM), jnp.float32))
    (key_acc, value_acc), query_blocks = lax.scan(
        block_step, start,
        (dec_query.reshape(blocks, TOK_DEV, width), ctx_grad.reshape(blocks, TOK_DEV, width), dec_segments.reshape(blocks, TOK_DEV)))
    query_grad = query_blocks.reshape(DEC, width)
    kv_grad = jnp.stack([key_acc.reshape(ENC, width), value_acc.reshape(ENC, width)], axis=1).astype(jnp.bfloat16)

    choose = (expert_ids.reshape(blocks, TOK_DEV)[:, :, None] == jnp.arange(EXPERTS, dtype=jnp.int32)[None, None, :]) & (keep_mask.reshape(blocks, TOK_DEV)[:, :, None] == 1)
    counts = jnp.cumsum(choose.astype(jnp.int32), axis=1) - 1
    slot_index = jnp.sum(jnp.where(choose, counts, 0), axis=2).astype(jnp.int32)
    routed = (jnp.any(choose, axis=2) & (slot_index < CAP)).reshape(DEC)
    position = (jnp.arange(blocks, dtype=jnp.int32)[:, None] * CAP + slot_index).reshape(DEC).astype(jnp.int32)
    slot_total = blocks * CAP
    token_index = jnp.arange(DEC, dtype=jnp.int32)
    input_grad = jnp.zeros((DEC, D), jnp.float32)
    gate_grad = jnp.zeros((DEC,), jnp.float32)
    in_grads = []
    out_grads = []
    for expert in range(EXPERTS):
        member = routed & (expert_ids == expert)
        where_to = jnp.where(member, position, slot_total).astype(jnp.int32)
        source = jnp.zeros((slot_total,), jnp.int32).at[where_to].set(token_index, mode="drop")
        filled = jnp.zeros((slot_total,), jnp.bool_).at[where_to].set(True, mode="drop")
        slot_input = jnp.where(filled[:, None], moe_input[source], jnp.zeros((), jnp.bfloat16))
        slot_grad = jnp.where(filled[:, None], moe_grad[source], jnp.zeros((), jnp.bfloat16))
        slot_gate = jnp.where(filled, gate_prob[source].astype(jnp.float32), jnp.zeros((), jnp.float32))
        w_in = w_input[:, expert * FF:(expert + 1) * FF]
        w_out = w_output[expert * FF:(expert + 1) * FF]
        pre_act = jnp.dot(slot_input, w_in, preferred_element_type=jnp.float32)
        back_hidden = jnp.dot(slot_grad, w_out.T, preferred_element_type=jnp.float32)
        active = jnp.maximum(pre_act, 0.0)
        hidden_grad = (slot_gate[:, None] * back_hidden * (pre_act > 0)).astype(jnp.bfloat16)
        scaled_hidden = (slot_gate[:, None] * active).astype(jnp.bfloat16)
        out_grads.append(jnp.dot(scaled_hidden.T, slot_grad, preferred_element_type=jnp.float32).astype(jnp.bfloat16))
        in_grads.append(jnp.dot(slot_input.T, hidden_grad, preferred_element_type=jnp.float32).astype(jnp.bfloat16))
        input_part = jnp.dot(hidden_grad, w_in.T, preferred_element_type=jnp.float32)
        gate_part = jnp.sum(active * back_hidden, axis=1)
        pick = jnp.minimum(where_to, slot_total - 1)
        input_grad = input_grad + jnp.where(member[:, None], input_part[pick], 0.0)
        gate_grad = gate_grad + jnp.where(member, gate_part[pick], 0.0)
    moe_input_grad = input_grad.astype(jnp.bfloat16)
    w_input_grad = jnp.concatenate(in_grads, axis=1)
    w_output_grad = jnp.concatenate(out_grads, axis=0)
    return (query_grad, kv_grad, moe_input_grad, gate_grad, w_input_grad, w_output_grad)
```

```python
import functools

import jax
import jax.numpy as jnp
from jax import lax
from jax.experimental import pallas as pl
from jax.experimental.pallas import tpu as pltpu
from jax.sharding import PartitionSpec as P

D = 4096
HEADS = 32
HEAD_DIM = 128
EXPERTS = 2
CAP = 10
SCALE = 0.125
NONE = -1e30
LANES = 128
BLOCK = 24
GATE_ROW = 20


def iota(shape, dim):
    return lax.broadcasted_iota(jnp.int32, shape, dim)


def one_hot(mask):
    return jnp.where(mask, 1.0, 0.0).astype(jnp.bfloat16)


def mm(a, b, dims=((1,), (0,))):
    return lax.dot_general(a, b, (dims, ((), ())), preferred_element_type=jnp.float32)


def slots_of(ids, keep, expert):
    tokens = ids.shape[1]
    row, col = iota((tokens, tokens), 0), iota((tokens, tokens), 1)
    chosen = (ids == expert) & (keep == 1)
    chosen_f = jnp.where(chosen, 1.0, 0.0)
    as_column = jnp.sum(jnp.where(row == col, chosen_f, 0.0), axis=1, keepdims=True)
    earlier = jnp.sum(jnp.where(row < col, as_column, 0.0), axis=0, keepdims=True)
    slot = earlier.astype(jnp.int32)
    return jnp.where(chosen & (slot < CAP), slot, -1)


def pack_kernel(mine, ids_ref, keep_ref, gate_ref, input_ref, grad_ref, own_ref, other_ref):
    ids, keep = ids_ref[...], keep_ref[...]
    tokens = ids.shape[1]
    gate = gate_ref[...].astype(jnp.float32)
    moe_input, moe_grad = input_ref[...], grad_ref[...]
    expert = mine()
    row = iota((BLOCK, tokens), 0)
    input_slot = jnp.where(row < 8, row, jnp.where((row == 16) | (row == 17), row - 8, -2))
    grad_slot = jnp.where(
        (row >= 8) & (row < 16), row - 8, jnp.where((row == 18) | (row == 19), row - 10, -2)
    )
    diagonal = iota((tokens, tokens), 0) == iota((tokens, tokens), 1)
    gate_column = jnp.sum(jnp.where(diagonal, gate, 0.0), axis=1, keepdims=True)
    for which, out_ref in ((expert, own_ref), (1 - expert, other_ref)):
        slot = slots_of(ids, keep, which)
        block = mm(one_hot(input_slot == slot), moe_input) + mm(one_hot(grad_slot == slot), moe_grad)
        slot_column = jnp.sum(jnp.where(diagonal, slot, 0), axis=1, keepdims=True)
        gates = jnp.sum(
            jnp.where(slot_column == iota((tokens, LANES), 1), gate_column, 0.0), axis=0, keepdims=True
        )
        out_ref[...] = block.astype(jnp.bfloat16)
        out_ref[:, :LANES] = (
            block[:, :LANES] + jnp.where(iota((BLOCK, LANES), 0) == GATE_ROW, gates, 0.0)
        ).astype(jnp.bfloat16)


def slot_rows(count):
    rows = iota((count * CAP, 1), 0)
    tail = rows - 8 * count
    source = jnp.where(rows < 8 * count, rows // 8, tail // 2)
    return source, jnp.where(rows < 8 * count, rows % 8, 8 + tail % 2)


def main_kernel(places, *refs):
    blocks = refs[: len(places)]
    w_in_ref, w_out_ref = refs[len(places) : len(places) + 2]
    x_out, g_out, hidden_ref, scaled_ref, keep_ref, send_ref = refs[len(places) + 2 : len(places) + 8]
    tails, gate_col, total, gate_part = refs[len(places) + 8 :]
    step, steps = pl.program_id(0), pl.num_programs(0)
    count = sum(r.shape[0] for r in blocks) * 2
    rows = count * CAP
    source, slot = slot_rows(count)

    @pl.when(step == 0)
    def _():
        for block, place in zip(blocks, places):
            for i in range(block.shape[0]):
                at = place + i
                first, second = block[i, 0], block[i, 1]
                x_out[pl.ds(16 * at, 16), :] = jnp.concatenate([first[:8], second[:8]], axis=0)
                g_out[pl.ds(16 * at, 16), :] = jnp.concatenate([first[8:16], second[8:16]], axis=0)
                tails[pl.ds(16 * at, 16), :] = jnp.concatenate([first[16:], second[16:]], axis=0)
        row, col = iota((2 * count, 8 * count), 0), iota((2 * count, 8 * count), 1)
        pick = 8 * (row // 2) + row % 2
        tail = tails[...]
        x_out[pl.ds(8 * count, 2 * count), :] = mm(one_hot(col == pick), tail).astype(jnp.bfloat16)
        g_out[pl.ds(8 * count, 2 * count), :] = mm(one_hot(col == pick + 2), tail).astype(jnp.bfloat16)
        of_row = one_hot(iota((rows, 8 * count), 1) == 8 * source + GATE_ROW - 16)
        gates = mm(of_row, tails[:, :LANES])
        gate_col[...] = jnp.sum(
            jnp.where(iota((rows, LANES), 1) == slot, gates, 0.0), axis=1, keepdims=True
        )
        total[...] = jnp.zeros_like(total)
        gate_part[...] = jnp.zeros_like(gate_part)

    w_in = w_in_ref[...]
    pre = mm(x_out[...], w_in)
    back = mm(g_out[...], w_out_ref[...], ((1,), (1,)))
    active = jnp.maximum(pre, 0.0)
    gate = gate_col[...]
    hidden = (gate * back * jnp.where(pre > 0, 1.0, 0.0)).astype(jnp.bfloat16)
    hidden_ref[...] = hidden
    scaled_ref[...] = (gate * active).astype(jnp.bfloat16)
    total[...] += mm(hidden, w_in, ((1,), (1,)))
    gate_part[...] += jnp.sum(active * back, axis=1, keepdims=True)

    @pl.when(step == steps - 1)
    def _():
        units = count // 2
        lane = iota((rows, LANES), 1)
        placed = jnp.where(lane == 16 * (source % 2) + slot, gate_part[...], 0.0).astype(jnp.bfloat16)
        low = total[pl.ds(8 * count, 2 * count), :].astype(jnp.bfloat16)
        row, col = iota((8 * units, 2 * count), 0), iota((8 * units, 2 * count), 1)
        ends = mm(one_hot((row % 8 < 4) & (col == 4 * (row // 8) + row % 8)), low)
        at = iota((8 * units, rows), 1)
        unit = jnp.where(at < 8 * count, at // 16, (at - 8 * count) // 4)
        row = iota((8 * units, rows), 0)
        gates = mm(one_hot((row % 8 == GATE_ROW - 16) & (unit == row // 8)), placed)
        for u in range(units):
            half, index = (keep_ref, u) if u < keep_ref.shape[0] else (send_ref, u - keep_ref.shape[0])
            half[index, :16, :] = total[pl.ds(16 * u, 16), :].astype(jnp.bfloat16)
            half[index, 16:, :] = ends[8 * u : 8 * u + 8].astype(jnp.bfloat16)
            half[index, 16:, :LANES] = (
                ends[8 * u : 8 * u + 8, :LANES] + gates[8 * u : 8 * u + 8]
            ).astype(jnp.bfloat16)


def sum_pairs_kernel(keep_ref, got_ref, own_ref, *out_refs):
    own_ref[...] = keep_ref[0].astype(jnp.float32) + got_ref[0].astype(jnp.float32)
    for i, out_ref in enumerate(out_refs):
        out_ref[...] = (
            keep_ref[i + 1].astype(jnp.float32) + got_ref[i + 1].astype(jnp.float32)
        ).astype(jnp.bfloat16)


def sum_unit_kernel(*refs):
    parts, (own_ref, send_ref) = refs[:-2], refs[-2:]
    unit = parts[0][...].astype(jnp.float32)
    for part in parts[1:]:
        unit = unit + part[...].astype(jnp.float32)
    own_ref[...] = unit
    send_ref[...] = unit[8:].astype(jnp.bfloat16)


def scatter_kernel(mine, ids_ref, keep_ref, own_ref, got_ref, grad_ref, gate_ref):
    ids, keep = ids_ref[...], keep_ref[...]
    tokens = ids.shape[1]
    expert = mine()
    diagonal = iota((tokens, tokens), 0) == iota((tokens, tokens), 1)
    own, got = own_ref[...], got_ref[...].astype(jnp.float32)
    grad = jnp.zeros((tokens, own.shape[1]), jnp.float32)
    gate = jnp.zeros((1, tokens), jnp.float32)
    for which, part, first, tail, lane in (
        (expert, own, 0, 16, 0),
        (1 - expert, got, 0, 10, 16),
    ):
        slot = slots_of(ids, keep, which)
        column = jnp.sum(jnp.where(diagonal, slot, 0), axis=1, keepdims=True)
        row = iota((tokens, part.shape[0]), 1)
        place = jnp.where(column < 8, first + column, tail + column - 8)
        grad = grad + mm(one_hot((row == place) & (column >= 0)), part.astype(jnp.bfloat16))
        gates = part[GATE_ROW - BLOCK + part.shape[0] :][:1, :LANES]
        wide = jnp.where(iota((LANES, tokens), 0) == slot + lane, 1.0, 0.0)
        wide = jnp.where(slot >= 0, wide, 0.0)
        column_gates = jnp.sum(
            jnp.where(iota((LANES, LANES), 0) == iota((LANES, LANES), 1), gates, 0.0), axis=1, keepdims=True
        )
        gate = gate + jnp.sum(wide * column_gates, axis=0, keepdims=True)
    grad_ref[...] = grad.astype(jnp.bfloat16)
    gate_ref[...] = gate


def params(limit=None):
    return pltpu.CompilerParams(vmem_limit_bytes=limit)


def expert_layer(moe_input, moe_grad, gate_prob, expert_ids, keep_mask, w_input, w_output):
    devices = lax.axis_size("seq")
    shards = devices // EXPERTS
    tokens = moe_input.shape[0]
    width = w_input.shape[1]

    def mine():
        return lax.axis_index("seq") // shards

    def flip(block, bits):
        return lax.ppermute(block, "seq", [(i, i ^ bits) for i in range(devices)])

    ids, keep = expert_ids.reshape(1, tokens), keep_mask.reshape(1, tokens)
    block_type = jax.ShapeDtypeStruct((BLOCK, D), jnp.bfloat16)
    own, other = pl.pallas_call(
        functools.partial(pack_kernel, mine), out_shape=(block_type, block_type), compiler_params=params()
    )(ids, keep, gate_prob.reshape(1, tokens), moe_input, moe_grad)
    across = (devices - 1) & ~3
    got = flip(other, across)
    pair = jnp.stack([own, got])[None]
    square = shards == 8
    if square:
        near = [pair, flip(pair, 2), flip(pair, 4), flip(pair, 6)]
        blocks = near + [flip(b, 1) for b in near]
    else:
        halves = [list(range(e * shards, (e + 1) * shards)) for e in range(EXPERTS)]
        blocks = [lax.all_gather(pair, "seq", axis_index_groups=halves, tiled=True)]
    places, at = [], 0
    for b in blocks:
        places.append(at)
        at += b.shape[0]
    sources = 2 * at
    rows = sources * CAP
    chunk = min(width, 256)
    keep_units = shards // 2
    slots = jax.ShapeDtypeStruct((rows, D), jnp.bfloat16)
    hidden_type = jax.ShapeDtypeStruct((rows, width), jnp.bfloat16)
    units_type = jax.ShapeDtypeStruct((keep_units, BLOCK, D), jnp.bfloat16)
    once = pl.Buffered(1)

    def whole(shape):
        return pl.BlockSpec(shape, lambda i: (0,) * len(shape), pipeline_mode=once)

    x, g, hidden, scaled, keep_half, send_half = pl.pallas_call(
        functools.partial(main_kernel, places),
        grid=(width // chunk,),
        in_specs=[whole(b.shape) for b in blocks]
        + [pl.BlockSpec((D, chunk), lambda i: (0, i)), pl.BlockSpec((chunk, D), lambda i: (i, 0))],
        out_specs=[
            whole(slots.shape),
            whole(slots.shape),
            pl.BlockSpec((rows, chunk), lambda i: (0, i)),
            pl.BlockSpec((rows, chunk), lambda i: (0, i)),
            whole(units_type.shape),
            whole(units_type.shape),
        ],
        out_shape=[slots, slots, hidden_type, hidden_type, units_type, units_type],
        scratch_shapes=[
            pltpu.VMEM((8 * sources, D), jnp.bfloat16),
            pltpu.VMEM((rows, 1), jnp.float32),
            pltpu.VMEM((rows, D), jnp.float32),
            pltpu.VMEM((rows, 1), jnp.float32),
        ],
        compiler_params=params(62 * 2**20 if not square else 48 * 2**20),
    )(*blocks, w_input, w_output)

    w_output_grad = mm(scaled, g, ((0,), (0,))).astype(jnp.bfloat16)
    w_input_grad = mm(x, hidden, ((0,), (0,))).astype(jnp.bfloat16)

    unit_wide = jax.ShapeDtypeStruct((BLOCK, D), jnp.float32)
    tail_type = jax.ShapeDtypeStruct((BLOCK - 8, D), jnp.bfloat16)
    if square:
        summed = pl.pallas_call(
            sum_pairs_kernel,
            out_shape=[unit_wide] + [block_type] * 3,
            compiler_params=params(),
        )(keep_half, flip(send_half, 1))
        parts = [summed[0], flip(summed[1], 2), flip(summed[2], 4), flip(summed[3], 6)]
    else:
        units = jnp.concatenate([keep_half, send_half]).astype(jnp.float32)
        parts = [
            lax.psum_scatter(units, "seq", axis_index_groups=halves, tiled=True).reshape(BLOCK, D)
        ]
    own_unit, send_unit = pl.pallas_call(
        sum_unit_kernel, out_shape=(unit_wide, tail_type), compiler_params=params()
    )(*parts)
    moe_input_grad, gate_grad = pl.pallas_call(
        functools.partial(scatter_kernel, mine),
        out_shape=(
            jax.ShapeDtypeStruct((tokens, D), jnp.bfloat16),
            jax.ShapeDtypeStruct((1, tokens), jnp.float32),
        ),
        compiler_params=params(),
    )(ids, keep, own_unit, flip(send_unit, across))
    return moe_input_grad, gate_grad.reshape(tokens), w_input_grad, w_output_grad


def token_kernel(query_ref, grad_ref, segments_ref, out_ref):
    tokens = query_ref.shape[0]
    out_ref[:tokens, :] = query_ref[...]
    out_ref[tokens : 2 * tokens, :] = grad_ref[...]
    out_ref[2 * tokens :, :] = jnp.zeros((8, out_ref.shape[1]), jnp.bfloat16)
    segments = segments_ref[...] + 1
    diagonal = iota((tokens, tokens), 0) == iota((tokens, tokens), 1)
    column = jnp.sum(jnp.where(diagonal, segments, 0), axis=1, keepdims=True)
    lane = iota((tokens, LANES), 1)
    row = iota((tokens, LANES), 0)
    digits = jnp.zeros((tokens, LANES), jnp.int32)
    for i in range(3):
        digits = digits + jnp.where(lane == row + i * tokens, (column >> (7 * i)) & 127, 0)
    line = jnp.sum(digits, axis=0, keepdims=True).astype(jnp.float32)
    out_ref[2 * tokens :, :LANES] = jnp.where(iota((8, LANES), 0) == 0, line, 0.0).astype(jnp.bfloat16)


def segment_column(token_ref, tokens):
    line = token_ref[2 * tokens :, :LANES][:1].astype(jnp.float32)
    lane, row = iota((tokens, LANES), 1), iota((tokens, LANES), 0)
    weight = jnp.zeros((tokens, LANES), jnp.float32)
    for i in range(3):
        weight = weight + jnp.where(lane == row + i * tokens, float(128**i), 0.0)
    return jnp.sum(weight * line, axis=1, keepdims=True).astype(jnp.int32)


def head_scores(token_refs, kv, head, tokens):
    lanes = pl.ds(head * HEAD_DIM, HEAD_DIM)
    queries = jnp.concatenate([r[:tokens, lanes] for r in token_refs], axis=0)
    grads = jnp.concatenate([r[tokens : 2 * tokens, lanes] for r in token_refs], axis=0)
    both = mm(jnp.concatenate([queries, grads], axis=0), kv, ((1,), (1,)))
    count = queries.shape[0]
    return queries, grads, both[:count], pltpu.roll(both[count:], both.shape[1] - 1, 1)


def allowed_pairs(token_refs, rows_ref, tokens):
    column = jnp.concatenate([segment_column(r, tokens) for r in token_refs], axis=0)
    rows = rows_ref[...]
    even = iota(rows.shape, 1) % 2 == 0
    return jnp.where(even, rows + 1, -1) == column


def load_head(kv_ref, head):
    rows = kv_ref.shape[0]
    return kv_ref[:, :, pl.ds(head * HEAD_DIM, HEAD_DIM)].reshape(2 * rows, HEAD_DIM)


def stats_kernel(own_ref, sib_ref, near_ref, rows_ref, kv_ref, stats_ref):
    token_refs = (own_ref, sib_ref, near_ref)
    tokens = (own_ref.shape[0] - 8) // 2
    allowed = allowed_pairs(token_refs, rows_ref, tokens)
    lane = iota((3 * tokens, LANES), 1)
    stats = jnp.zeros((3 * tokens, LANES), jnp.float32)
    for head in range(HEADS):
        _, _, scores, prob_grad = head_scores(token_refs, load_head(kv_ref, head), head, tokens)
        scores = jnp.where(allowed, SCALE * scores, NONE)
        peak = jnp.max(scores, axis=1, keepdims=True)
        weight = jnp.where(allowed, jnp.exp(scores - peak), 0.0)
        mass = jnp.sum(weight, axis=1, keepdims=True)
        delta = jnp.sum(weight * prob_grad, axis=1, keepdims=True)
        stats = jnp.where(lane == head, peak, stats)
        stats = jnp.where(lane == HEADS + head, mass, stats)
        stats = jnp.where(lane == 2 * HEADS + head, delta, stats)
    stats_ref[...] = stats


def merged(parts):
    peaks = [jnp.where(p[:, HEADS : 2 * HEADS] > 0, p[:, :HEADS], NONE) for p in parts]
    peak = jnp.maximum(jnp.maximum(peaks[0], peaks[1]), peaks[2])
    scale = [jnp.exp(p - peak) for p in peaks]
    mass = sum(s * p[:, HEADS : 2 * HEADS] for s, p in zip(scale, parts))
    delta = sum(s * p[:, 2 * HEADS : 3 * HEADS] for s, p in zip(scale, parts))
    inverse = jnp.where(mass > 0, 1.0 / mass, 0.0)
    return peak, inverse, delta * inverse


def grads_kernel(
    own_ref, sib_ref, near_ref, rows_ref, kv_ref, st_ref, st_sib_ref, st_near_ref, st_far_ref, st_side_ref,
    query_ref, to_sib_ref, to_near_ref, kv_grad_ref,
):
    token_refs = (own_ref, sib_ref, near_ref)
    tokens = (own_ref.shape[0] - 8) // 2
    allowed = allowed_pairs(token_refs, rows_ref, tokens)
    a, b, c = slice(0, tokens), slice(tokens, 2 * tokens), slice(2 * tokens, 3 * tokens)
    totals = [
        merged((st_ref[a], st_sib_ref[b], st_near_ref[c])),
        merged((st_ref[b], st_sib_ref[a], st_side_ref[c])),
        merged((st_ref[c], st_near_ref[a], st_far_ref[b])),
    ]
    peak, scale, delta = (jnp.concatenate([t[i] for t in totals], axis=0) for i in range(3))
    for head in range(HEADS):
        kv = load_head(kv_ref, head)
        queries, grads, scores, prob_grad = head_scores(token_refs, kv, head, tokens)
        at = slice(head, head + 1)
        probs = jnp.exp(jnp.where(allowed, SCALE * scores - peak[:, at], NONE)) * scale[:, at]
        score_grad = SCALE * (probs * (prob_grad - delta[:, at]))
        moved = pltpu.roll(probs, 1, 1)
        score_low = score_grad.astype(jnp.bfloat16)
        query = mm(score_low, kv)
        lanes = pl.ds(head * HEAD_DIM, HEAD_DIM)
        query_ref[:, lanes] = query[a]
        to_sib_ref[:, lanes] = query[b].astype(jnp.bfloat16)
        to_near_ref[:, lanes] = query[c].astype(jnp.bfloat16)
        both = jnp.concatenate([score_low, moved.astype(jnp.bfloat16)], axis=0)
        grad = mm(both, jnp.concatenate([queries, grads], axis=0), ((0,), (0,)))
        kv_grad_ref[:, :, lanes] = grad.astype(jnp.bfloat16).reshape(kv_grad_ref.shape[0], 2, HEAD_DIM)


def attention(dec_query, ctx_grad, dec_segments, enc_kv, enc_segments):
    devices = lax.axis_size("seq")
    tokens = dec_query.shape[0]
    rows = enc_kv.shape[0]
    crossing = [(i, i + 1) for i in range(1, devices - 1, 2)]

    def core(block):
        return lax.ppermute(block, "seq", [(i, i ^ 1) for i in range(devices)])

    def cross(block):
        return lax.ppermute(block, "seq", crossing + [(j, i) for i, j in crossing])

    own = pl.pallas_call(
        token_kernel,
        out_shape=jax.ShapeDtypeStruct((2 * tokens + 8, D), jnp.bfloat16),
        compiler_params=params(),
    )(dec_query, ctx_grad, dec_segments.reshape(1, tokens))
    held = (own, core(own), cross(own), jnp.repeat(enc_segments, 2).reshape(1, 2 * rows), enc_kv)
    stats_type = jax.ShapeDtypeStruct((3 * tokens, LANES), jnp.float32)
    stats = pl.pallas_call(stats_kernel, out_shape=stats_type, compiler_params=params(32 * 2**20))(*held)
    stats_sib, stats_near = core(stats), cross(stats)
    low = jax.ShapeDtypeStruct((tokens, D), jnp.bfloat16)
    query, to_sib, to_near, kv_grad = pl.pallas_call(
        grads_kernel,
        out_shape=(
            jax.ShapeDtypeStruct((tokens, D), jnp.float32), low, low,
            jax.ShapeDtypeStruct(enc_kv.shape, jnp.bfloat16),
        ),
        compiler_params=params(32 * 2**20),
    )(*held, stats, stats_sib, stats_near, cross(stats_sib), core(stats_near))
    query_grad = query + core(to_sib).astype(jnp.float32) + cross(to_near).astype(jnp.float32)
    return query_grad.astype(jnp.bfloat16), kv_grad


def local(
    dec_query,
    ctx_grad,
    dec_segments,
    enc_kv,
    enc_segments,
    moe_input,
    moe_grad,
    gate_prob,
    expert_ids,
    keep_mask,
    w_input,
    w_output,
):
    query_grad, kv_grad = attention(dec_query, ctx_grad, dec_segments, enc_kv, enc_segments)
    moe_input_grad, gate_grad, w_input_grad, w_output_grad = expert_layer(
        moe_input, moe_grad, gate_prob, expert_ids, keep_mask, w_input, w_output
    )
    return (query_grad, kv_grad, moe_input_grad, gate_grad, w_input_grad, w_output_grad)


def solution(mesh):
    return jax.shard_map(
        local,
        mesh=mesh,
        in_specs=(
            P(("groups", "seq"), None),
            P(("groups", "seq"), None),
            P(("groups", "seq")),
            P(("groups", "seq"), None, None),
            P(("groups", "seq")),
            P(("groups", "seq"), None),
            P(("groups", "seq"), None),
            P(("groups", "seq")),
            P(("groups", "seq")),
            P(("groups", "seq")),
            P(None, "seq"),
            P("seq", None),
        ),
        out_specs=(
            P(("groups", "seq"), None),
            P(("groups", "seq"), None, None),
            P(("groups", "seq"), None),
            P(("groups", "seq")),
            P("groups", "seq"),
            P("seq", "groups"),
        ),
        check_vma=False,
    )
```

```python
import functools

import jax
import jax.numpy as jnp
from jax import lax
from jax.experimental import pallas as pl
from jax.experimental.pallas import tpu as pltpu
from jax.sharding import PartitionSpec as P

D = 4096
HEADS = 32
HEAD_DIM = 128
EXPERTS = 2
CAP = 10
SCALE = 0.125
NONE = -1e30
LANES = 128
BLOCK = 24
GATE_ROW = 20
PIECE = 512
MAIN_LIMIT = 14 * 2**20
SMALL_LIMIT = 56 * 2**20


def iota(shape, dim):
    return lax.broadcasted_iota(jnp.int32, shape, dim)


def one_hot(mask):
    return jnp.where(mask, 1.0, 0.0).astype(jnp.bfloat16)


def mm(a, b, dims=((1,), (0,))):
    return lax.dot_general(a, b, (dims, ((), ())), preferred_element_type=jnp.float32)


def slots_of(ids, keep, expert):
    tokens = ids.shape[1]
    row, col = iota((tokens, tokens), 0), iota((tokens, tokens), 1)
    chosen = (ids == expert) & (keep == 1)
    chosen_f = jnp.where(chosen, 1.0, 0.0)
    as_column = jnp.sum(jnp.where(row == col, chosen_f, 0.0), axis=1, keepdims=True)
    earlier = jnp.sum(jnp.where(row < col, as_column, 0.0), axis=0, keepdims=True)
    slot = earlier.astype(jnp.int32)
    return jnp.where(chosen & (slot < CAP), slot, -1)


def pack_kernel(
    mine, ids_ref, keep_ref, gate_ref, input_ref, grad_ref, query_ref, ctx_ref, segments_ref,
    own_ref, other_ref, tokens_ref,
):
    pack_tokens(query_ref, ctx_ref, segments_ref, tokens_ref)
    ids, keep = ids_ref[...], keep_ref[...]
    tokens = ids.shape[1]
    gate = gate_ref[...].astype(jnp.float32)
    moe_input, moe_grad = input_ref[...], grad_ref[...]
    expert = mine()
    row = iota((BLOCK, tokens), 0)
    input_slot = jnp.where(row < 8, row, jnp.where((row == 16) | (row == 17), row - 8, -2))
    grad_slot = jnp.where(
        (row >= 8) & (row < 16), row - 8, jnp.where((row == 18) | (row == 19), row - 10, -2)
    )
    diagonal = iota((tokens, tokens), 0) == iota((tokens, tokens), 1)
    gate_column = jnp.sum(jnp.where(diagonal, gate, 0.0), axis=1, keepdims=True)
    for which, out_ref in ((expert, own_ref), (1 - expert, other_ref)):
        slot = slots_of(ids, keep, which)
        block = mm(one_hot(input_slot == slot), moe_input) + mm(one_hot(grad_slot == slot), moe_grad)
        slot_column = jnp.sum(jnp.where(diagonal, slot, 0), axis=1, keepdims=True)
        gates = jnp.sum(
            jnp.where(slot_column == iota((tokens, LANES), 1), gate_column, 0.0), axis=0, keepdims=True
        )
        out_ref[...] = block.astype(jnp.bfloat16)
        out_ref[:, :LANES] = (
            block[:, :LANES] + jnp.where(iota((BLOCK, LANES), 0) == GATE_ROW, gates, 0.0)
        ).astype(jnp.bfloat16)


def slot_rows(count):
    rows = iota((count * CAP, 1), 0)
    tail = rows - 8 * count
    source = jnp.where(rows < 8 * count, rows // 8, tail // 2)
    return source, jnp.where(rows < 8 * count, rows % 8, 8 + tail % 2)


def main_kernel(places, *refs):
    blocks, refs = refs[: len(places)], refs[len(places) :]
    w_in_ref, w_out_ref, x_out, g_out, hidden_ref, scaled_ref, keep_ref, send_ref = refs[:8]
    (tails,) = refs[8:]
    count = sum(r.shape[0] for r in blocks) * 2
    rows = count * CAP
    units = count // 2
    width = w_in_ref.shape[1]
    chunk = min(width, 256)
    source, slot = slot_rows(count)
    for block, place in zip(blocks, places):
        for i in range(block.shape[0]):
            at = place + i
            first, second = block[i, 0], block[i, 1]
            x_out[pl.ds(16 * at, 16), :] = jnp.concatenate([first[:8], second[:8]], axis=0)
            g_out[pl.ds(16 * at, 16), :] = jnp.concatenate([first[8:16], second[8:16]], axis=0)
            tails[pl.ds(16 * at, 16), :] = jnp.concatenate([first[16:], second[16:]], axis=0)
    row, col = iota((2 * count, 8 * count), 0), iota((2 * count, 8 * count), 1)
    pick = 8 * (row // 2) + row % 2
    tail = tails[...]
    x_out[pl.ds(8 * count, 2 * count), :] = mm(one_hot(col == pick), tail).astype(jnp.bfloat16)
    g_out[pl.ds(8 * count, 2 * count), :] = mm(one_hot(col == pick + 2), tail).astype(jnp.bfloat16)
    of_row = one_hot(iota((rows, 8 * count), 1) == 8 * source + GATE_ROW - 16)
    gates = mm(of_row, tails[:, :LANES])
    gate = jnp.sum(jnp.where(iota((rows, LANES), 1) == slot, gates, 0.0), axis=1, keepdims=True)

    gate_part = jnp.zeros((rows, 1), jnp.float32)
    for i in range(width // chunk):
        at = pl.ds(i * chunk, chunk)
        pre = mm(x_out[...], w_in_ref[:, at])
        back = mm(g_out[...], w_out_ref[at, :], ((1,), (1,)))
        active = jnp.maximum(pre, 0.0)
        hidden_ref[:, at] = (gate * back * jnp.where(pre > 0, 1.0, 0.0)).astype(jnp.bfloat16)
        scaled_ref[:, at] = (gate * active).astype(jnp.bfloat16)
        gate_part += jnp.sum(active * back, axis=1, keepdims=True)

    lane = iota((rows, LANES), 1)
    placed = jnp.where(lane == 16 * (source % 2) + slot, gate_part, 0.0).astype(jnp.bfloat16)
    at = iota((8 * units, rows), 1)
    unit = jnp.where(at < 8 * count, at // 16, (at - 8 * count) // 4)
    row = iota((8 * units, rows), 0)
    gates = mm(one_hot((row % 8 == GATE_ROW - 16) & (unit == row // 8)), placed)
    row, col = iota((8 * units, 2 * count), 0), iota((8 * units, 2 * count), 1)
    to_end = one_hot((row % 8 < 4) & (col == 4 * (row // 8) + row % 8))
    hidden = hidden_ref[...]
    for start in range(0, D, PIECE):
        lanes = pl.ds(start, PIECE)
        part = mm(hidden, w_in_ref[lanes, :], ((1,), (1,))).astype(jnp.bfloat16)
        ends = mm(to_end, part[8 * count :])
        if start == 0:
            ends = jnp.concatenate([ends[:, :LANES] + gates, ends[:, LANES:]], axis=1)
        ends = ends.astype(jnp.bfloat16)
        for u in range(units):
            half, index = (keep_ref, u) if u < keep_ref.shape[0] else (send_ref, u - keep_ref.shape[0])
            half[index, :16, lanes] = part[16 * u : 16 * u + 16]
            half[index, 16:, lanes] = ends[8 * u : 8 * u + 8]


def weights_kernel(x_ref, hidden_ref, scaled_ref, g_ref, w_in_ref, w_out_ref):
    w_in_ref[...] = mm(x_ref[...], hidden_ref[...], ((0,), (0,))).astype(jnp.bfloat16)
    w_out_ref[...] = mm(scaled_ref[...], g_ref[...], ((0,), (0,))).astype(jnp.bfloat16)


def sum_pairs_kernel(keep_ref, got_ref, own_ref, *out_refs):
    own_ref[...] = keep_ref[0].astype(jnp.float32) + got_ref[0].astype(jnp.float32)
    for i, out_ref in enumerate(out_refs):
        out_ref[...] = (
            keep_ref[i + 1].astype(jnp.float32) + got_ref[i + 1].astype(jnp.float32)
        ).astype(jnp.bfloat16)


def sum_unit_kernel(*refs):
    parts, (own_ref, send_ref) = refs[:-2], refs[-2:]
    unit = parts[0][...].astype(jnp.float32)
    for part in parts[1:]:
        unit = unit + part[...].astype(jnp.float32)
    own_ref[...] = unit
    send_ref[...] = unit[8:].astype(jnp.bfloat16)


def scatter_kernel(mine, ids_ref, keep_ref, own_ref, got_ref, grad_ref, gate_ref):
    ids, keep = ids_ref[...], keep_ref[...]
    tokens = ids.shape[1]
    expert = mine()
    diagonal = iota((tokens, tokens), 0) == iota((tokens, tokens), 1)
    own, got = own_ref[...], got_ref[...].astype(jnp.float32)
    grad = jnp.zeros((tokens, own.shape[1]), jnp.float32)
    gate = jnp.zeros((1, tokens), jnp.float32)
    for which, part, first, tail, lane in (
        (expert, own, 0, 16, 0),
        (1 - expert, got, 0, 10, 16),
    ):
        slot = slots_of(ids, keep, which)
        column = jnp.sum(jnp.where(diagonal, slot, 0), axis=1, keepdims=True)
        row = iota((tokens, part.shape[0]), 1)
        place = jnp.where(column < 8, first + column, tail + column - 8)
        grad = grad + mm(one_hot((row == place) & (column >= 0)), part.astype(jnp.bfloat16))
        gates = part[GATE_ROW - BLOCK + part.shape[0] :][:1, :LANES]
        wide = jnp.where(iota((LANES, tokens), 0) == slot + lane, 1.0, 0.0)
        wide = jnp.where(slot >= 0, wide, 0.0)
        column_gates = jnp.sum(
            jnp.where(iota((LANES, LANES), 0) == iota((LANES, LANES), 1), gates, 0.0), axis=1, keepdims=True
        )
        gate = gate + jnp.sum(wide * column_gates, axis=0, keepdims=True)
    grad_ref[...] = grad.astype(jnp.bfloat16)
    gate_ref[...] = gate


def params(limit=4 * 2**20):
    return pltpu.CompilerParams(vmem_limit_bytes=limit)


def pack_tokens(query_ref, grad_ref, segments_ref, out_ref):
    tokens = query_ref.shape[0]
    out_ref[:tokens, :] = query_ref[...]
    out_ref[tokens : 2 * tokens, :] = grad_ref[...]
    out_ref[2 * tokens :, :] = jnp.zeros((8, out_ref.shape[1]), jnp.bfloat16)
    segments = segments_ref[...] + 1
    diagonal = iota((tokens, tokens), 0) == iota((tokens, tokens), 1)
    column = jnp.sum(jnp.where(diagonal, segments, 0), axis=1, keepdims=True)
    lane = iota((tokens, LANES), 1)
    row = iota((tokens, LANES), 0)
    digits = jnp.zeros((tokens, LANES), jnp.int32)
    for i in range(3):
        digits = digits + jnp.where(lane == row + i * tokens, (column >> (7 * i)) & 127, 0)
    line = jnp.sum(digits, axis=0, keepdims=True).astype(jnp.float32)
    out_ref[2 * tokens :, :LANES] = jnp.where(iota((8, LANES), 0) == 0, line, 0.0).astype(jnp.bfloat16)


def segment_column(token_ref, tokens):
    line = token_ref[2 * tokens :, :LANES][:1].astype(jnp.float32)
    lane, row = iota((tokens, LANES), 1), iota((tokens, LANES), 0)
    weight = jnp.zeros((tokens, LANES), jnp.float32)
    for i in range(3):
        weight = weight + jnp.where(lane == row + i * tokens, float(128**i), 0.0)
    return jnp.sum(weight * line, axis=1, keepdims=True).astype(jnp.int32)


def head_scores(token_refs, kv, head, tokens):
    lanes = pl.ds(head * HEAD_DIM, HEAD_DIM)
    queries = jnp.concatenate([r[:tokens, lanes] for r in token_refs], axis=0)
    grads = jnp.concatenate([r[tokens : 2 * tokens, lanes] for r in token_refs], axis=0)
    both = mm(jnp.concatenate([queries, grads], axis=0), kv, ((1,), (1,)))
    count = queries.shape[0]
    return queries, grads, both[:count], pltpu.roll(both[count:], both.shape[1] - 1, 1)


def allowed_pairs(token_refs, rows_ref, tokens):
    column = jnp.concatenate([segment_column(r, tokens) for r in token_refs], axis=0)
    rows = rows_ref[...] + 1
    count = rows.shape[1]
    diagonal = iota((count, count), 0) == iota((count, count), 1)
    as_column = jnp.sum(jnp.where(diagonal, rows, 0), axis=1, keepdims=True)
    even = iota((count, 2 * count), 1) == 2 * iota((count, 2 * count), 0)
    spread = jnp.sum(jnp.where(even, as_column, 0), axis=0, keepdims=True)
    return jnp.where(spread > 0, spread, -1) == column


def load_head(kv_ref, head):
    rows = kv_ref.shape[0]
    return kv_ref[:, :, pl.ds(head * HEAD_DIM, HEAD_DIM)].reshape(2 * rows, HEAD_DIM)


def stats_kernel(own_ref, sib_ref, near_ref, rows_ref, kv_ref, stats_ref):
    token_refs = (own_ref, sib_ref, near_ref)
    tokens = (own_ref.shape[0] - 8) // 2
    allowed = allowed_pairs(token_refs, rows_ref, tokens)
    lane = iota((3 * tokens, LANES), 1)
    stats = jnp.zeros((3 * tokens, LANES), jnp.float32)
    for head in range(HEADS):
        _, _, scores, prob_grad = head_scores(token_refs, load_head(kv_ref, head), head, tokens)
        scores = jnp.where(allowed, SCALE * scores, NONE)
        peak = jnp.max(scores, axis=1, keepdims=True)
        weight = jnp.where(allowed, jnp.exp(scores - peak), 0.0)
        mass = jnp.sum(weight, axis=1, keepdims=True)
        delta = jnp.sum(weight * prob_grad, axis=1, keepdims=True)
        stats = jnp.where(lane == head, peak, stats)
        stats = jnp.where(lane == HEADS + head, mass, stats)
        stats = jnp.where(lane == 2 * HEADS + head, delta, stats)
    stats_ref[...] = stats


def merged(parts):
    peaks = [jnp.where(p[:, HEADS : 2 * HEADS] > 0, p[:, :HEADS], NONE) for p in parts]
    peak = jnp.maximum(jnp.maximum(peaks[0], peaks[1]), peaks[2])
    scale = [jnp.exp(p - peak) for p in peaks]
    mass = sum(s * p[:, HEADS : 2 * HEADS] for s, p in zip(scale, parts))
    delta = sum(s * p[:, 2 * HEADS : 3 * HEADS] for s, p in zip(scale, parts))
    inverse = jnp.where(mass > 0, 1.0 / mass, 0.0)
    return peak, inverse, delta * inverse


def grads_kernel(
    own_ref, sib_ref, near_ref, rows_ref, kv_ref, st_ref, st_sib_ref, st_near_ref, st_far_ref, st_side_ref,
    query_ref, to_sib_ref, to_near_ref, kv_grad_ref,
):
    token_refs = (own_ref, sib_ref, near_ref)
    tokens = (own_ref.shape[0] - 8) // 2
    allowed = allowed_pairs(token_refs, rows_ref, tokens)
    a, b, c = slice(0, tokens), slice(tokens, 2 * tokens), slice(2 * tokens, 3 * tokens)
    totals = [
        merged((st_ref[a], st_sib_ref[b], st_near_ref[c])),
        merged((st_ref[b], st_sib_ref[a], st_side_ref[c])),
        merged((st_ref[c], st_near_ref[a], st_far_ref[b])),
    ]
    peak, scale, delta = (jnp.concatenate([t[i] for t in totals], axis=0) for i in range(3))
    for head in range(HEADS):
        kv = load_head(kv_ref, head)
        queries, grads, scores, prob_grad = head_scores(token_refs, kv, head, tokens)
        at = slice(head, head + 1)
        probs = jnp.exp(jnp.where(allowed, SCALE * scores - peak[:, at], NONE)) * scale[:, at]
        score_grad = SCALE * (probs * (prob_grad - delta[:, at]))
        moved = pltpu.roll(probs, 1, 1)
        score_low = score_grad.astype(jnp.bfloat16)
        query = mm(score_low, kv)
        lanes = pl.ds(head * HEAD_DIM, HEAD_DIM)
        query_ref[:, lanes] = query[a]
        to_sib_ref[:, lanes] = query[b].astype(jnp.bfloat16)
        to_near_ref[:, lanes] = query[c].astype(jnp.bfloat16)
        both = jnp.concatenate([score_low, moved.astype(jnp.bfloat16)], axis=0)
        grad = mm(both, jnp.concatenate([queries, grads], axis=0), ((0,), (0,)))
        kv_grad_ref[:, :, lanes] = grad.astype(jnp.bfloat16).reshape(kv_grad_ref.shape[0], 2, HEAD_DIM)


def core(block):
    return lax.ppermute(block, "seq", [(i, i ^ 1) for i in range(lax.axis_size("seq"))])


def cross(block):
    crossing = [(i, i + 1) for i in range(1, lax.axis_size("seq") - 1, 2)]
    return lax.ppermute(block, "seq", crossing + [(j, i) for i, j in crossing])


def attention_stats(held):
    tokens = (held[0].shape[0] - 8) // 2
    return pl.pallas_call(
        stats_kernel,
        out_shape=jax.ShapeDtypeStruct((3 * tokens, LANES), jnp.float32),
        compiler_params=params(12 * 2**20),
        cost_estimate=pl.CostEstimate(flops=10**9, bytes_accessed=16 * 10**6, transcendentals=0),
    )(*held)


def attention_grads(held, stats):
    tokens = (held[0].shape[0] - 8) // 2
    low = jax.ShapeDtypeStruct((tokens, D), jnp.bfloat16)
    return pl.pallas_call(
        grads_kernel,
        out_shape=(
            jax.ShapeDtypeStruct((tokens, D), jnp.float32),
            low,
            low,
            jax.ShapeDtypeStruct(held[-1].shape, jnp.bfloat16),
        ),
        compiler_params=params(12 * 2**20),
        cost_estimate=pl.CostEstimate(flops=10**9, bytes_accessed=32 * 10**6, transcendentals=0),
    )(*held, *stats)


def after(value, *others):
    return lax.optimization_barrier((value, *others))[0]


def far(value):
    return pltpu.with_memory_space_constraint(value, pltpu.HBM)


def fetch_kernel(count, *refs):
    arrived = refs[2 * count]
    copies = [
        pltpu.make_async_copy(refs[i], refs[count + i], arrived.at[i]) for i in range(count)
    ]
    for copy in copies:
        copy.start()
    for copy in copies:
        copy.wait()


def fetch(*arrays):
    return pl.pallas_call(
        functools.partial(fetch_kernel, len(arrays)),
        in_specs=[pl.BlockSpec(memory_space=pltpu.HBM)] * len(arrays),
        out_specs=[pl.BlockSpec(memory_space=pltpu.VMEM)] * len(arrays),
        out_shape=[jax.ShapeDtypeStruct(a.shape, a.dtype) for a in arrays],
        scratch_shapes=[pltpu.SemaphoreType.DMA((len(arrays),))],
        compiler_params=params(24 * 2**20),
        cost_estimate=pl.CostEstimate(
            flops=0, bytes_accessed=sum(a.size * 2 for a in arrays), transcendentals=0
        ),
    )(*map(far, arrays))


def local(
    dec_query,
    ctx_grad,
    dec_segments,
    enc_kv,
    enc_segments,
    moe_input,
    moe_grad,
    gate_prob,
    expert_ids,
    keep_mask,
    w_input,
    w_output,
):
    devices = lax.axis_size("seq")
    shards = devices // EXPERTS
    tokens = moe_input.shape[0]
    width = w_input.shape[1]
    square = shards == 8

    def mine():
        return lax.axis_index("seq") // shards

    def flip(block, bits):
        return lax.ppermute(block, "seq", [(i, i ^ bits) for i in range(devices)])

    ids, keep = expert_ids.reshape(1, tokens), keep_mask.reshape(1, tokens)
    block_type = jax.ShapeDtypeStruct((BLOCK, D), jnp.bfloat16)
    own, other, packed = pl.pallas_call(
        functools.partial(pack_kernel, mine),
        out_shape=(block_type, block_type, jax.ShapeDtypeStruct((2 * tokens + 8, D), jnp.bfloat16)),
        compiler_params=params(8 * 2**20),
    )(
        *map(far, (ids, keep, gate_prob.reshape(1, tokens), moe_input, moe_grad)),
        *map(far, (dec_query, ctx_grad, dec_segments.reshape(1, tokens))),
    )
    across = (devices - 1) & ~3
    got = flip(other, across)
    near_w_input, near_w_output, near_kv = w_input, w_output, enc_kv
    if square:
        near_w_input, near_w_output, near_kv = fetch(w_input, w_output, enc_kv)
    held = (packed, core(packed), cross(packed), far(enc_segments.reshape(1, -1)), near_kv)
    stats = attention_stats(held)
    stats_sib, stats_near = core(stats), cross(stats)

    pair = jnp.stack([own, got])
    if square:
        pair = after(pair, held[1], held[2], near_w_input)
        near = [pair, flip(pair, 2), flip(pair, 4), flip(pair, 6)]
        *near, stats, stats_sib, stats_near = lax.optimization_barrier(
            (*near, stats, stats_sib, stats_near)
        )
        blocks = [b[None] for b in near + [flip(b, 1) for b in near]]
    else:
        halves = [list(range(e * shards, (e + 1) * shards)) for e in range(EXPERTS)]
        blocks = [lax.all_gather(pair[None], "seq", axis_index_groups=halves, tiled=True)]
    places, at = [], 0
    for b in blocks:
        places.append(at)
        at += b.shape[0]
    sources = 2 * at
    rows = sources * CAP
    keep_units = shards // 2
    slots = jax.ShapeDtypeStruct((rows, D), jnp.bfloat16)
    hidden_type = jax.ShapeDtypeStruct((rows, width), jnp.bfloat16)
    units_type = jax.ShapeDtypeStruct((keep_units, BLOCK, D), jnp.bfloat16)
    x, g, hidden, scaled, keep_half, send_half = pl.pallas_call(
        functools.partial(main_kernel, places),
        out_shape=[slots, slots, hidden_type, hidden_type, units_type, units_type],
        in_specs=[pl.BlockSpec(memory_space=pltpu.VMEM)] * len(places)
        + [pl.BlockSpec(memory_space=pltpu.VMEM)] * 2,
        scratch_shapes=[pltpu.VMEM((8 * sources, D), jnp.bfloat16)],
        compiler_params=params(MAIN_LIMIT if square else 62 * 2**20),
        cost_estimate=pl.CostEstimate(flops=6 * rows * D * width, bytes_accessed=4 * D * width, transcendentals=0),
    )(*blocks, near_w_input, near_w_output)

    unit_wide = jax.ShapeDtypeStruct((BLOCK, D), jnp.float32)
    tail_type = jax.ShapeDtypeStruct((BLOCK - 8, D), jnp.bfloat16)
    if square:
        swapped = flip(send_half, 1)
        stats_sib, stats_near = after((stats_sib, stats_near), keep_half)
        stats_far, stats_side = cross(stats_sib), core(stats_near)
        summed = pl.pallas_call(
            sum_pairs_kernel,
            out_shape=[unit_wide] + [block_type] * 3,
            compiler_params=params(),
        )(keep_half, swapped)
        parts = [summed[0], flip(summed[1], 2), flip(summed[2], 4), flip(summed[3], 6)]
        all_stats = after((stats, stats_sib, stats_near, stats_far, stats_side), summed[0])
    else:
        units = jnp.concatenate([keep_half, send_half]).astype(jnp.float32)
        parts = [
            lax.psum_scatter(units, "seq", axis_index_groups=halves, tiled=True).reshape(BLOCK, D)
        ]
        all_stats = (stats, stats_sib, stats_near, cross(stats_sib), core(stats_near))
    query, to_sib, to_near, kv_grad = attention_grads(held, all_stats)
    parts[0] = after(parts[0], query)
    own_unit, send_unit = pl.pallas_call(
        sum_unit_kernel, out_shape=(unit_wide, tail_type), compiler_params=params()
    )(*parts)
    returned = flip(send_unit, across)
    to_sib, to_near = after((to_sib, to_near), own_unit)
    query_grad = query + core(to_sib).astype(jnp.float32) + cross(to_near).astype(jnp.float32)

    x, hidden, scaled, g = after((x, hidden, scaled, g), own_unit)
    pieces = max(1, min(4, width // 128))
    once = pl.Buffered(1)
    w_input_grad, w_output_grad = pl.pallas_call(
        weights_kernel,
        grid=(pieces,),
        in_specs=[
            pl.BlockSpec((rows, D // pieces), lambda i: (0, i)),
            pl.BlockSpec((rows, width), lambda i: (0, 0), pipeline_mode=once),
            pl.BlockSpec((rows, width // pieces), lambda i: (0, i)),
            pl.BlockSpec((rows, D), lambda i: (0, 0), pipeline_mode=once),
        ],
        out_specs=[
            pl.BlockSpec((D // pieces, width), lambda i: (i, 0)),
            pl.BlockSpec((width // pieces, D), lambda i: (i, 0)),
        ],
        out_shape=[
            jax.ShapeDtypeStruct((D, width), jnp.bfloat16),
            jax.ShapeDtypeStruct((width, D), jnp.bfloat16),
        ],
        compiler_params=params(24 * 2**20),
        cost_estimate=pl.CostEstimate(flops=4 * rows * D * width, bytes_accessed=4 * D * width, transcendentals=0),
    )(x, hidden, scaled, g)

    moe_input_grad, gate_grad = pl.pallas_call(
        functools.partial(scatter_kernel, mine),
        out_shape=(
            jax.ShapeDtypeStruct((tokens, D), jnp.bfloat16),
            jax.ShapeDtypeStruct((1, tokens), jnp.float32),
        ),
        compiler_params=params(),
    )(ids, keep, own_unit, returned)
    return (
        query_grad.astype(jnp.bfloat16),
        kv_grad,
        moe_input_grad,
        gate_grad.reshape(tokens),
        w_input_grad,
        w_output_grad,
    )


def solution(mesh):
    return jax.shard_map(
        local,
        mesh=mesh,
        in_specs=(
            P(("groups", "seq"), None),
            P(("groups", "seq"), None),
            P(("groups", "seq")),
            P(("groups", "seq"), None, None),
            P(("groups", "seq")),
            P(("groups", "seq"), None),
            P(("groups", "seq"), None),
            P(("groups", "seq")),
            P(("groups", "seq")),
            P(("groups", "seq")),
            P(None, "seq"),
            P("seq", None),
        ),
        out_specs=(
            P(("groups", "seq"), None),
            P(("groups", "seq"), None, None),
            P(("groups", "seq"), None),
            P(("groups", "seq")),
            P("groups", "seq"),
            P("seq", "groups"),
        ),
        check_vma=False,
    )
```

```python
import functools

import jax
import jax.numpy as jnp
from jax import lax
from jax.experimental import pallas as pl
from jax.experimental.pallas import tpu as pltpu
from jax.sharding import PartitionSpec as P

D = 4096
HEADS = 32
HEAD_DIM = 128
EXPERTS = 2
CAP = 10
SCALE = 0.125
NONE = -1e30
LANES = 128
FOLD = D // 4
WIDE = D + FOLD + LANES
TAILS = slice(D, D + FOLD)
SIDE = slice(D + FOLD, WIDE)
MAIN_LIMIT = 24 * 2**20


def iota(shape, dim):
    return lax.broadcasted_iota(jnp.int32, shape, dim)


def one_hot(mask):
    return jnp.where(mask, 1.0, 0.0).astype(jnp.bfloat16)


def mm(a, b, dims=((1,), (0,))):
    return lax.dot_general(a, b, (dims, ((), ())), preferred_element_type=jnp.float32)


def slots_of(ids, keep, expert):
    tokens = ids.shape[1]
    row, col = iota((tokens, tokens), 0), iota((tokens, tokens), 1)
    chosen = (ids == expert) & (keep == 1)
    chosen_f = jnp.where(chosen, 1.0, 0.0)
    as_column = jnp.sum(jnp.where(row == col, chosen_f, 0.0), axis=1, keepdims=True)
    earlier = jnp.sum(jnp.where(row < col, as_column, 0.0), axis=0, keepdims=True)
    slot = earlier.astype(jnp.int32)
    return jnp.where(chosen & (slot < CAP), slot, -1)


def pack_kernel(
    mine, ids_ref, keep_ref, gate_ref, input_ref, grad_ref, query_ref, ctx_ref, segments_ref,
    own_ref, other_ref, tokens_ref,
):
    pack_tokens(query_ref, ctx_ref, segments_ref, tokens_ref)
    ids, keep = ids_ref[...], keep_ref[...]
    tokens = ids.shape[1]
    gate = gate_ref[...].astype(jnp.float32)
    moe_input, moe_grad = input_ref[...], grad_ref[...]
    expert = mine()
    row = iota((24, tokens), 0)
    input_slot = jnp.where(row < 8, row, jnp.where((row == 16) | (row == 17), row - 8, -2))
    grad_slot = jnp.where(
        (row >= 8) & (row < 16), row - 8, jnp.where((row == 18) | (row == 19), row - 10, -2)
    )
    gate_slot = jnp.where(row < CAP, row, -2)
    for which, out_ref in ((expert, own_ref), (1 - expert, other_ref)):
        slot = slots_of(ids, keep, which)
        block = mm(one_hot(input_slot == slot), moe_input) + mm(one_hot(grad_slot == slot), moe_grad)
        block = block.astype(jnp.bfloat16)
        out_ref[:, :D] = block[:16]
        for b in range(4):
            out_ref[4 * b : 4 * b + 4, TAILS] = block[16:20, b * FOLD : (b + 1) * FOLD]
        gates = jnp.sum(jnp.where(gate_slot == slot, gate, 0.0), axis=1, keepdims=True)
        out_ref[:, SIDE] = jnp.broadcast_to(gates[:16], (16, LANES)).astype(jnp.bfloat16)


def main_kernel(places, *refs):
    blocks, refs = refs[: len(places)], refs[len(places) :]
    w_in_ref, w_out_far, x_out, g_out, hidden_ref, scaled_ref, keep_ref, send_ref = refs[:8]
    tails, gate_ref, pre_ref, w_out_ref, arrived = refs[8:]
    fetched = pltpu.make_async_copy(w_out_far, w_out_ref, arrived)
    fetched.start()
    units = sum(r.shape[0] for r in blocks)
    heads, rows = 16 * units, 20 * units
    width = w_in_ref.shape[1]
    chunk = min(width, 256)
    for block, place in zip(blocks, places):
        for i in range(block.shape[0]):
            at = place + i
            pair = block[i]
            both = jnp.concatenate([pair[:8], pair[16:24]], axis=0)
            x_out[pl.ds(16 * at, 16), :] = both[:, :D]
            gate_ref[pl.ds(16 * at, 16), :] = both[:, SIDE].astype(jnp.float32)
            g_out[pl.ds(16 * at, 16), :] = jnp.concatenate([pair[8:16, :D], pair[24:32, :D]], axis=0)
            gate_ref[pl.ds(heads + 4 * at, 4), :] = jnp.concatenate(
                [pair[8:10, SIDE], pair[24:26, SIDE]], axis=0
            ).astype(jnp.float32)
            for b in range(4):
                tails[pl.ds(8 * at, 8), pl.ds(b * FOLD, FOLD)] = jnp.concatenate(
                    [pair[4 * b : 4 * b + 4, TAILS], pair[16 + 4 * b : 20 + 4 * b, TAILS]], axis=0
                )
    row, col = iota((4 * units, 8 * units), 0), iota((4 * units, 8 * units), 1)
    pick = 4 * (row // 2) + row % 2
    tail = tails[...]
    x_out[pl.ds(heads, 4 * units), :] = mm(one_hot(col == pick), tail).astype(jnp.bfloat16)
    g_out[pl.ds(heads, 4 * units), :] = mm(one_hot(col == pick + 2), tail).astype(jnp.bfloat16)
    gate = gate_ref[:, :1]

    for start in range(0, width, chunk):
        at = pl.ds(start, chunk)
        pre_ref[:, at] = mm(x_out[...], w_in_ref[:, at])
    fetched.wait()
    gate_part = jnp.zeros((rows, 1), jnp.float32)
    for start in range(0, width, chunk):
        at = pl.ds(start, chunk)
        pre = pre_ref[:, at]
        back = mm(g_out[...], w_out_ref[at, :], ((1,), (1,)))
        active = jnp.maximum(pre, 0.0)
        hidden_ref[:, at] = (gate * back * jnp.where(pre > 0, 1.0, 0.0)).astype(jnp.bfloat16)
        scaled_ref[:, at] = (gate * active).astype(jnp.bfloat16)
        gate_part += jnp.sum(active * back, axis=1, keepdims=True)

    halves = [(keep_ref, u) for u in range(keep_ref.shape[0])] + [(send_ref, u) for u in range(send_ref.shape[0])]
    hidden = hidden_ref[...]
    for b in range(4):
        lanes = pl.ds(b * FOLD, FOLD)
        part = mm(hidden, w_in_ref[lanes, :], ((1,), (1,))).astype(jnp.bfloat16)
        for u, (half, index) in enumerate(halves):
            half[index, :, lanes] = part[16 * u : 16 * u + 16]
            half[index, 4 * b : 4 * b + 4, TAILS] = part[heads + 4 * u : heads + 4 * u + 4]
    lane = iota((16, LANES), 1)
    for u, (half, index) in enumerate(halves):
        ends = gate_part[heads + 4 * u : heads + 4 * u + 4]
        ends = jnp.concatenate([ends, jnp.zeros((12, 1), jnp.float32)], axis=0)
        side = jnp.where(lane == 0, gate_part[16 * u : 16 * u + 16], jnp.where(lane == 1, ends, 0.0))
        half[index, :, SIDE] = side.astype(jnp.bfloat16)


def weights_kernel(x_ref, hidden_ref, scaled_ref, g_ref, w_in_ref, w_out_ref):
    w_in_ref[...] = mm(x_ref[...], hidden_ref[...], ((0,), (0,))).astype(jnp.bfloat16)
    w_out_ref[...] = mm(scaled_ref[...], g_ref[...], ((0,), (0,))).astype(jnp.bfloat16)


def sum_pairs_kernel(keep_ref, got_ref, own_ref, *out_refs):
    own_ref[...] = keep_ref[0].astype(jnp.float32) + got_ref[0].astype(jnp.float32)
    for i, out_ref in enumerate(out_refs):
        out_ref[...] = (
            keep_ref[i + 1].astype(jnp.float32) + got_ref[i + 1].astype(jnp.float32)
        ).astype(jnp.bfloat16)


def sum_unit_kernel(*refs):
    parts, (own_ref, send_ref) = refs[:-2], refs[-2:]
    unit = parts[0][...].astype(jnp.float32)
    for part in parts[1:]:
        unit = unit + part[...].astype(jnp.float32)
    own_ref[...] = unit
    low = unit.astype(jnp.bfloat16)
    send_ref[:, :D] = low[8:, :D]
    for b in range(4):
        send_ref[2 * b : 2 * b + 2, TAILS] = low[4 * b + 2 : 4 * b + 4, TAILS]
    lane = iota((8, LANES), 1)
    ends = jnp.concatenate([unit[2:4, SIDE], jnp.zeros((6, LANES), jnp.float32)], axis=0)
    send_ref[:, SIDE] = jnp.where(lane == 0, unit[8:, SIDE], ends).astype(jnp.bfloat16)


def scatter_kernel(mine, ids_ref, keep_ref, own_ref, got_ref, grad_ref, gate_ref):
    ids, keep = ids_ref[...], keep_ref[...]
    tokens = ids.shape[1]
    expert = mine()
    diagonal = iota((tokens, tokens), 0) == iota((tokens, tokens), 1)
    own, got = own_ref[...], got_ref[...].astype(jnp.float32)
    grad = jnp.zeros((tokens, D), jnp.float32)
    gate = jnp.zeros((1, tokens), jnp.float32)
    for which, part, step in ((expert, own, 4), (1 - expert, got, 2)):
        slot = slots_of(ids, keep, which)
        column = jnp.sum(jnp.where(diagonal, slot, 0), axis=1, keepdims=True)
        ends = jnp.concatenate([part[step * b : step * b + 2, TAILS] for b in range(4)], axis=1)
        full = jnp.concatenate([part[:8, :D], ends, jnp.zeros((6, D), jnp.float32)], axis=0)
        grad = grad + mm(one_hot(iota((tokens, 16), 1) == column), full.astype(jnp.bfloat16))
        side = part[:, SIDE]
        gates = jnp.concatenate([side[:8, :1], side[:2, 1:2], jnp.zeros((6, 1), jnp.float32)], axis=0)
        gate = gate + jnp.sum(jnp.where(iota((16, tokens), 0) == slot, gates, 0.0), axis=0, keepdims=True)
    grad_ref[...] = grad.astype(jnp.bfloat16)
    gate_ref[...] = gate


def params(limit=4 * 2**20):
    return pltpu.CompilerParams(vmem_limit_bytes=limit)


def pack_tokens(query_ref, grad_ref, segments_ref, out_ref):
    tokens = query_ref.shape[0]
    out_ref[:tokens, :D] = query_ref[...]
    out_ref[tokens:, :D] = grad_ref[...]
    segments = segments_ref[...] + 1
    diagonal = iota((tokens, tokens), 0) == iota((tokens, tokens), 1)
    column = jnp.sum(jnp.where(diagonal, segments, 0), axis=1, keepdims=True)
    lane = iota((tokens, LANES), 1)
    digits = jnp.zeros((tokens, LANES), jnp.int32)
    for i in range(3):
        digits = digits + jnp.where(lane == i, (column >> (7 * i)) & 127, 0)
    out_ref[:tokens, D:] = digits.astype(jnp.float32).astype(jnp.bfloat16)
    out_ref[tokens:, D:] = jnp.zeros((tokens, LANES), jnp.bfloat16)


def segment_column(token_ref, tokens):
    digits = token_ref[:tokens, D:].astype(jnp.float32)
    lane = iota((tokens, LANES), 1)
    weight = jnp.zeros((tokens, LANES), jnp.float32)
    for i in range(3):
        weight = weight + jnp.where(lane == i, float(128**i), 0.0)
    return jnp.sum(weight * digits, axis=1, keepdims=True).astype(jnp.int32)


def head_scores(token_refs, kv, head, tokens):
    lanes = pl.ds(head * HEAD_DIM, HEAD_DIM)
    queries = jnp.concatenate([r[:tokens, lanes] for r in token_refs], axis=0)
    grads = jnp.concatenate([r[tokens : 2 * tokens, lanes] for r in token_refs], axis=0)
    both = mm(jnp.concatenate([queries, grads], axis=0), kv, ((1,), (1,)))
    count = queries.shape[0]
    return queries, grads, both[:count], pltpu.roll(both[count:], both.shape[1] - 1, 1)


def allowed_pairs(token_refs, rows_ref, tokens):
    column = jnp.concatenate([segment_column(r, tokens) for r in token_refs], axis=0)
    rows = rows_ref[...] + 1
    count = rows.shape[1]
    diagonal = iota((count, count), 0) == iota((count, count), 1)
    as_column = jnp.sum(jnp.where(diagonal, rows, 0), axis=1, keepdims=True)
    even = iota((count, 2 * count), 1) == 2 * iota((count, 2 * count), 0)
    spread = jnp.sum(jnp.where(even, as_column, 0), axis=0, keepdims=True)
    return jnp.where(spread > 0, spread, -1) == column


def load_head(kv_ref, head):
    rows = kv_ref.shape[0]
    return kv_ref[:, :, pl.ds(head * HEAD_DIM, HEAD_DIM)].reshape(2 * rows, HEAD_DIM)


def stats_kernel(own_ref, sib_ref, near_ref, rows_ref, kv_ref, stats_ref):
    token_refs = (own_ref, sib_ref, near_ref)
    tokens = own_ref.shape[0] // 2
    allowed = allowed_pairs(token_refs, rows_ref, tokens)
    lane = iota((3 * tokens, LANES), 1)
    stats = jnp.zeros((3 * tokens, LANES), jnp.float32)
    for head in range(HEADS):
        _, _, scores, prob_grad = head_scores(token_refs, load_head(kv_ref, head), head, tokens)
        scores = jnp.where(allowed, SCALE * scores, NONE)
        peak = jnp.max(scores, axis=1, keepdims=True)
        weight = jnp.where(allowed, jnp.exp(scores - peak), 0.0)
        mass = jnp.sum(weight, axis=1, keepdims=True)
        delta = jnp.sum(weight * prob_grad, axis=1, keepdims=True)
        stats = jnp.where(lane == head, peak, stats)
        stats = jnp.where(lane == HEADS + head, mass, stats)
        stats = jnp.where(lane == 2 * HEADS + head, delta, stats)
    stats_ref[...] = stats


def merged(parts):
    peaks = [jnp.where(p[:, HEADS : 2 * HEADS] > 0, p[:, :HEADS], NONE) for p in parts]
    peak = jnp.maximum(jnp.maximum(peaks[0], peaks[1]), peaks[2])
    scale = [jnp.exp(p - peak) for p in peaks]
    mass = sum(s * p[:, HEADS : 2 * HEADS] for s, p in zip(scale, parts))
    delta = sum(s * p[:, 2 * HEADS : 3 * HEADS] for s, p in zip(scale, parts))
    inverse = jnp.where(mass > 0, 1.0 / mass, 0.0)
    return peak, inverse, delta * inverse


def grads_kernel(
    own_ref, sib_ref, near_ref, rows_ref, kv_ref, st_ref, st_sib_ref, met_ref, sib_met_ref,
    query_ref, to_sib_ref, to_near_ref, kv_grad_ref,
):
    token_refs = (own_ref, sib_ref, near_ref)
    tokens = own_ref.shape[0] // 2
    allowed = allowed_pairs(token_refs, rows_ref, tokens)
    a, b, c = slice(0, tokens), slice(tokens, 2 * tokens), slice(2 * tokens, 3 * tokens)
    far_b = slice(4 * tokens, 5 * tokens)
    totals = [
        merged((st_ref[a], st_sib_ref[b], met_ref[c])),
        merged((st_ref[b], st_sib_ref[a], sib_met_ref[c])),
        merged((st_ref[c], met_ref[a], met_ref[far_b])),
    ]
    peak, scale, delta = (jnp.concatenate([t[i] for t in totals], axis=0) for i in range(3))
    for head in range(HEADS):
        kv = load_head(kv_ref, head)
        queries, grads, scores, prob_grad = head_scores(token_refs, kv, head, tokens)
        at = slice(head, head + 1)
        probs = jnp.exp(jnp.where(allowed, SCALE * scores - peak[:, at], NONE)) * scale[:, at]
        score_grad = SCALE * (probs * (prob_grad - delta[:, at]))
        moved = pltpu.roll(probs, 1, 1)
        score_low = score_grad.astype(jnp.bfloat16)
        query = mm(score_low, kv)
        lanes = pl.ds(head * HEAD_DIM, HEAD_DIM)
        query_ref[:, lanes] = query[a]
        to_sib_ref[:, lanes] = query[b].astype(jnp.bfloat16)
        to_near_ref[:, lanes] = query[c].astype(jnp.bfloat16)
        both = jnp.concatenate([score_low, moved.astype(jnp.bfloat16)], axis=0)
        grad = mm(both, jnp.concatenate([queries, grads], axis=0), ((0,), (0,)))
        kv_grad_ref[:, :, lanes] = grad.astype(jnp.bfloat16).reshape(kv_grad_ref.shape[0], 2, HEAD_DIM)


def core(block):
    return lax.ppermute(block, "seq", [(i, i ^ 1) for i in range(lax.axis_size("seq"))])


def cross(block):
    crossing = [(i, i + 1) for i in range(1, lax.axis_size("seq") - 1, 2)]
    return lax.ppermute(block, "seq", crossing + [(j, i) for i, j in crossing])


def attention_stats(held):
    tokens = held[0].shape[0] // 2
    return pl.pallas_call(
        stats_kernel,
        out_shape=jax.ShapeDtypeStruct((3 * tokens, LANES), jnp.float32),
        compiler_params=params(12 * 2**20),
        cost_estimate=pl.CostEstimate(flops=10**9, bytes_accessed=16 * 10**6, transcendentals=0),
    )(*held)


def attention_grads(held, stats):
    tokens = held[0].shape[0] // 2
    low = jax.ShapeDtypeStruct((tokens, D), jnp.bfloat16)
    return pl.pallas_call(
        grads_kernel,
        out_shape=(
            jax.ShapeDtypeStruct((tokens, D), jnp.float32),
            low,
            low,
            jax.ShapeDtypeStruct(held[-1].shape, jnp.bfloat16),
        ),
        compiler_params=params(12 * 2**20),
        cost_estimate=pl.CostEstimate(flops=10**9, bytes_accessed=32 * 10**6, transcendentals=0),
    )(*held, *stats)


def after(value, *others):
    return lax.optimization_barrier((value, *others))[0]


def far(value):
    return pltpu.with_memory_space_constraint(value, pltpu.HBM)


def fetch_kernel(count, *refs):
    arrived = refs[2 * count]
    copies = [
        pltpu.make_async_copy(refs[i], refs[count + i], arrived.at[i]) for i in range(count)
    ]
    for copy in copies:
        copy.start()
    for copy in copies:
        copy.wait()


def fetch(*arrays):
    return pl.pallas_call(
        functools.partial(fetch_kernel, len(arrays)),
        in_specs=[pl.BlockSpec(memory_space=pltpu.HBM)] * len(arrays),
        out_specs=[pl.BlockSpec(memory_space=pltpu.VMEM)] * len(arrays),
        out_shape=[jax.ShapeDtypeStruct(a.shape, a.dtype) for a in arrays],
        scratch_shapes=[pltpu.SemaphoreType.DMA((len(arrays),))],
        compiler_params=params(24 * 2**20),
        cost_estimate=pl.CostEstimate(
            flops=0, bytes_accessed=sum(a.size * 2 for a in arrays), transcendentals=0
        ),
    )(*map(far, arrays))


def local(
    dec_query,
    ctx_grad,
    dec_segments,
    enc_kv,
    enc_segments,
    moe_input,
    moe_grad,
    gate_prob,
    expert_ids,
    keep_mask,
    w_input,
    w_output,
):
    devices = lax.axis_size("seq")
    shards = devices // EXPERTS
    tokens = moe_input.shape[0]
    width = w_input.shape[1]
    square = shards == 8

    def mine():
        return lax.axis_index("seq") // shards

    def flip(block, bits):
        return lax.ppermute(block, "seq", [(i, i ^ bits) for i in range(devices)])

    ids, keep = expert_ids.reshape(1, tokens), keep_mask.reshape(1, tokens)
    block_type = jax.ShapeDtypeStruct((16, WIDE), jnp.bfloat16)
    sent_type = jax.ShapeDtypeStruct((16, WIDE), jnp.bfloat16)
    own, other, packed = pl.pallas_call(
        functools.partial(pack_kernel, mine),
        out_shape=(sent_type, sent_type, jax.ShapeDtypeStruct((2 * tokens, D + LANES), jnp.bfloat16)),
        compiler_params=params(8 * 2**20),
    )(
        *map(far, (ids, keep, gate_prob.reshape(1, tokens), moe_input, moe_grad)),
        *map(far, (dec_query, ctx_grad, dec_segments.reshape(1, tokens))),
    )
    across = (devices - 1) & ~3
    got = flip(other, across)
    near_w_input, near_kv = w_input, enc_kv
    if square:
        near_w_input, near_kv = fetch(w_input, enc_kv)
    held = (packed, core(packed), cross(packed), far(enc_segments.reshape(1, -1)), near_kv)
    stats = attention_stats(held)
    stats_sib = core(stats)
    met = cross(jnp.concatenate([stats, stats_sib]))
    all_stats = (stats, stats_sib, met, core(met))

    pair = jnp.concatenate([own, got])
    if square:
        pair = after(pair, held[1], held[2], near_kv)
        near = [pair, flip(pair, 2), flip(pair, 4), flip(pair, 6)]
        beside = flip(pair, 1)
        *near, all_stats = lax.optimization_barrier((*near, all_stats))
        blocks = [b[None] for b in near + [beside] + [flip(b, 1) for b in near[1:]]]
    else:
        halves = [list(range(e * shards, (e + 1) * shards)) for e in range(EXPERTS)]
        blocks = [lax.all_gather(pair[None], "seq", axis_index_groups=halves, tiled=True)]
    places, at = [], 0
    for b in blocks:
        places.append(at)
        at += b.shape[0]
    sources = 2 * at
    rows = sources * CAP
    keep_units = shards // 2
    slots = jax.ShapeDtypeStruct((rows, D), jnp.bfloat16)
    hidden_type = jax.ShapeDtypeStruct((rows, width), jnp.bfloat16)
    units_type = jax.ShapeDtypeStruct((keep_units, 16, WIDE), jnp.bfloat16)
    x, g, hidden, scaled, keep_half, send_half = pl.pallas_call(
        functools.partial(main_kernel, places),
        out_shape=[slots, slots, hidden_type, hidden_type, units_type, units_type],
        in_specs=[pl.BlockSpec(memory_space=pltpu.VMEM)] * len(places)
        + [pl.BlockSpec(memory_space=pltpu.VMEM), pl.BlockSpec(memory_space=pltpu.HBM)],
        scratch_shapes=[
            pltpu.VMEM((4 * sources, D), jnp.bfloat16),
            pltpu.VMEM((rows, LANES), jnp.float32),
            pltpu.VMEM((rows, width), jnp.float32),
            pltpu.VMEM((width, D), jnp.bfloat16),
            pltpu.SemaphoreType.DMA,
        ],
        compiler_params=params(MAIN_LIMIT if square else 62 * 2**20),
        cost_estimate=pl.CostEstimate(flops=6 * rows * D * width, bytes_accessed=4 * D * width, transcendentals=0),
    )(*blocks, near_w_input, far(w_output))

    unit_wide = jax.ShapeDtypeStruct((16, WIDE), jnp.float32)
    tail_type = jax.ShapeDtypeStruct((8, WIDE), jnp.bfloat16)
    if square:
        swapped = flip(send_half, 1)
        summed = pl.pallas_call(
            sum_pairs_kernel,
            out_shape=[unit_wide] + [block_type] * 3,
            compiler_params=params(),
        )(keep_half, swapped)
        parts = [summed[0], flip(summed[1], 2), flip(summed[2], 4), flip(summed[3], 6)]
        all_stats = after(all_stats, summed[0])
    else:
        units = jnp.concatenate([keep_half, send_half]).astype(jnp.float32)
        parts = [
            lax.psum_scatter(units, "seq", axis_index_groups=halves, tiled=True).reshape(16, WIDE)
        ]
    query, to_sib, to_near, kv_grad = attention_grads(held, all_stats)
    parts[0] = after(parts[0], query)
    own_unit, send_unit = pl.pallas_call(
        sum_unit_kernel, out_shape=(unit_wide, tail_type), compiler_params=params()
    )(*parts)
    returned = flip(send_unit, across)
    to_sib, to_near = after((to_sib, to_near), own_unit)
    query_grad = query + core(to_sib).astype(jnp.float32) + cross(to_near).astype(jnp.float32)

    x, hidden, scaled, g = after((x, hidden, scaled, g), own_unit)
    pieces = max(1, min(4, width // 128))
    once = pl.Buffered(1)
    w_input_grad, w_output_grad = pl.pallas_call(
        weights_kernel,
        grid=(pieces,),
        in_specs=[
            pl.BlockSpec((rows, D // pieces), lambda i: (0, i)),
            pl.BlockSpec((rows, width), lambda i: (0, 0), pipeline_mode=once),
            pl.BlockSpec((rows, width // pieces), lambda i: (0, i)),
            pl.BlockSpec((rows, D), lambda i: (0, 0), pipeline_mode=once),
        ],
        out_specs=[
            pl.BlockSpec((D // pieces, width), lambda i: (i, 0)),
            pl.BlockSpec((width // pieces, D), lambda i: (i, 0)),
        ],
        out_shape=[
            jax.ShapeDtypeStruct((D, width), jnp.bfloat16),
            jax.ShapeDtypeStruct((width, D), jnp.bfloat16),
        ],
        compiler_params=params(24 * 2**20),
        cost_estimate=pl.CostEstimate(flops=4 * rows * D * width, bytes_accessed=4 * D * width, transcendentals=0),
    )(x, hidden, scaled, g)

    moe_input_grad, gate_grad = pl.pallas_call(
        functools.partial(scatter_kernel, mine),
        out_shape=(
            jax.ShapeDtypeStruct((tokens, D), jnp.bfloat16),
            jax.ShapeDtypeStruct((1, tokens), jnp.float32),
        ),
        compiler_params=params(),
    )(ids, keep, own_unit, returned)
    return (
        query_grad.astype(jnp.bfloat16),
        kv_grad,
        moe_input_grad,
        gate_grad.reshape(tokens),
        w_input_grad,
        w_output_grad,
    )


def solution(mesh):
    return jax.shard_map(
        local,
        mesh=mesh,
        in_specs=(
            P(("groups", "seq"), None),
            P(("groups", "seq"), None),
            P(("groups", "seq")),
            P(("groups", "seq"), None, None),
            P(("groups", "seq")),
            P(("groups", "seq"), None),
            P(("groups", "seq"), None),
            P(("groups", "seq")),
            P(("groups", "seq")),
            P(("groups", "seq")),
            P(None, "seq"),
            P("seq", None),
        ),
        out_specs=(
            P(("groups", "seq"), None),
            P(("groups", "seq"), None, None),
            P(("groups", "seq"), None),
            P(("groups", "seq")),
            P("groups", "seq"),
            P("seq", "groups"),
        ),
        check_vma=False,
    )
```

```python
import functools

import jax
import jax.numpy as jnp
from jax import lax
from jax.experimental import pallas as pl
from jax.experimental.pallas import tpu as pltpu
from jax.sharding import PartitionSpec as P

D = 4096
HEADS = 32
HEAD_DIM = 128
EXPERTS = 2
CAP = 10
SCALE = 0.125
NONE = -1e30
LANES = 128
FOLD = D // 4
WIDE = D + FOLD + LANES
TAILS = slice(D, D + FOLD)
SIDE = slice(D + FOLD, WIDE)
GROUP = 4
MAIN_LIMIT = 24 * 2**20


def iota(shape, dim):
    return lax.broadcasted_iota(jnp.int32, shape, dim)


def one_hot(mask):
    return jnp.where(mask, 1.0, 0.0).astype(jnp.bfloat16)


def mm(a, b, dims=((1,), (0,))):
    return lax.dot_general(a, b, (dims, ((), ())), preferred_element_type=jnp.float32)


def slots_of(ids, keep, expert):
    tokens = ids.shape[1]
    row, col = iota((tokens, tokens), 0), iota((tokens, tokens), 1)
    chosen = (ids == expert) & (keep == 1)
    chosen_f = jnp.where(chosen, 1.0, 0.0)
    as_column = jnp.sum(jnp.where(row == col, chosen_f, 0.0), axis=1, keepdims=True)
    earlier = jnp.sum(jnp.where(row < col, as_column, 0.0), axis=0, keepdims=True)
    slot = earlier.astype(jnp.int32)
    return jnp.where(chosen & (slot < CAP), slot, -1)


def pack_kernel(
    mine, ids_ref, keep_ref, gate_ref, input_ref, grad_ref, query_ref, ctx_ref, segments_ref,
    own_ref, other_ref, tokens_ref,
):
    pack_tokens(query_ref, ctx_ref, segments_ref, tokens_ref)
    ids, keep = ids_ref[...], keep_ref[...]
    tokens = ids.shape[1]
    gate = gate_ref[...].astype(jnp.float32)
    moe_input, moe_grad = input_ref[...], grad_ref[...]
    expert = mine()
    row = iota((24, tokens), 0)
    input_slot = jnp.where(row < 8, row, jnp.where((row == 16) | (row == 17), row - 8, -2))
    grad_slot = jnp.where(
        (row >= 8) & (row < 16), row - 8, jnp.where((row == 18) | (row == 19), row - 10, -2)
    )
    gate_slot = jnp.where(row < CAP, row, -2)
    for which, out_ref in ((expert, own_ref), (1 - expert, other_ref)):
        slot = slots_of(ids, keep, which)
        block = mm(one_hot(input_slot == slot), moe_input) + mm(one_hot(grad_slot == slot), moe_grad)
        block = block.astype(jnp.bfloat16)
        out_ref[:, :D] = block[:16]
        for b in range(4):
            out_ref[4 * b : 4 * b + 4, TAILS] = block[16:20, b * FOLD : (b + 1) * FOLD]
        gates = jnp.sum(jnp.where(gate_slot == slot, gate, 0.0), axis=1, keepdims=True)
        out_ref[:, SIDE] = jnp.broadcast_to(gates[:16], (16, LANES)).astype(jnp.bfloat16)


def main_kernel(places, *refs):
    blocks, refs = refs[: len(places)], refs[len(places) :]
    w_in_ref, w_out_far, x_out, g_out, hidden_ref, scaled_ref, keep_ref, send_ref = refs[:8]
    tails, gate_ref, pre_ref, w_out_ref, arrived = refs[8:]
    fetched = pltpu.make_async_copy(w_out_far, w_out_ref, arrived)
    fetched.start()
    units = sum(r.shape[0] for r in blocks)
    heads, rows = 16 * units, 20 * units
    width = w_in_ref.shape[1]
    chunk = min(width, 256)
    for block, place in zip(blocks, places):
        for i in range(block.shape[0]):
            at = place + i
            pair = block[i]
            both = jnp.concatenate([pair[:8], pair[16:24]], axis=0)
            x_out[pl.ds(16 * at, 16), :] = both[:, :D]
            gate_ref[pl.ds(16 * at, 16), :] = both[:, SIDE].astype(jnp.float32)
            g_out[pl.ds(16 * at, 16), :] = jnp.concatenate([pair[8:16, :D], pair[24:32, :D]], axis=0)
            gate_ref[pl.ds(heads + 4 * at, 4), :] = jnp.concatenate(
                [pair[8:10, SIDE], pair[24:26, SIDE]], axis=0
            ).astype(jnp.float32)
            for b in range(4):
                tails[pl.ds(8 * at, 8), pl.ds(b * FOLD, FOLD)] = jnp.concatenate(
                    [pair[4 * b : 4 * b + 4, TAILS], pair[16 + 4 * b : 20 + 4 * b, TAILS]], axis=0
                )
    row, col = iota((4 * units, 8 * units), 0), iota((4 * units, 8 * units), 1)
    pick = 4 * (row // 2) + row % 2
    tail = tails[...]
    x_out[pl.ds(heads, 4 * units), :] = mm(one_hot(col == pick), tail).astype(jnp.bfloat16)
    g_out[pl.ds(heads, 4 * units), :] = mm(one_hot(col == pick + 2), tail).astype(jnp.bfloat16)
    gate = gate_ref[:, :1]

    for start in range(0, width, chunk):
        at = pl.ds(start, chunk)
        pre_ref[:, at] = mm(x_out[...], w_in_ref[:, at])
    fetched.wait()
    gate_part = jnp.zeros((rows, 1), jnp.float32)
    for start in range(0, width, chunk):
        at = pl.ds(start, chunk)
        pre = pre_ref[:, at]
        back = mm(g_out[...], w_out_ref[at, :], ((1,), (1,)))
        active = jnp.maximum(pre, 0.0)
        hidden_ref[:, at] = (gate * back * jnp.where(pre > 0, 1.0, 0.0)).astype(jnp.bfloat16)
        scaled_ref[:, at] = (gate * active).astype(jnp.bfloat16)
        gate_part += jnp.sum(active * back, axis=1, keepdims=True)

    halves = [(keep_ref, u) for u in range(keep_ref.shape[0])] + [(send_ref, u) for u in range(send_ref.shape[0])]
    hidden = hidden_ref[...]
    for b in range(4):
        lanes = pl.ds(b * FOLD, FOLD)
        part = mm(hidden, w_in_ref[lanes, :], ((1,), (1,))).astype(jnp.bfloat16)
        for u, (half, index) in enumerate(halves):
            half[index, :, lanes] = part[16 * u : 16 * u + 16]
            half[index, 4 * b : 4 * b + 4, TAILS] = part[heads + 4 * u : heads + 4 * u + 4]
    lane = iota((16, LANES), 1)
    for u, (half, index) in enumerate(halves):
        ends = gate_part[heads + 4 * u : heads + 4 * u + 4]
        ends = jnp.concatenate([ends, jnp.zeros((12, 1), jnp.float32)], axis=0)
        side = jnp.where(lane == 0, gate_part[16 * u : 16 * u + 16], jnp.where(lane == 1, ends, 0.0))
        half[index, :, SIDE] = side.astype(jnp.bfloat16)


def weights_kernel(x_ref, hidden_ref, scaled_ref, g_ref, w_in_ref, w_out_ref):
    w_in_ref[...] = mm(x_ref[...], hidden_ref[...], ((0,), (0,))).astype(jnp.bfloat16)
    w_out_ref[...] = mm(scaled_ref[...], g_ref[...], ((0,), (0,))).astype(jnp.bfloat16)


def sum_pairs_kernel(keep_ref, got_ref, own_ref, *out_refs):
    own_ref[...] = keep_ref[0].astype(jnp.float32) + got_ref[0].astype(jnp.float32)
    for i, out_ref in enumerate(out_refs):
        out_ref[...] = (
            keep_ref[i + 1].astype(jnp.float32) + got_ref[i + 1].astype(jnp.float32)
        ).astype(jnp.bfloat16)


def sum_unit_kernel(*refs):
    parts, (own_ref, send_ref) = refs[:-2], refs[-2:]
    unit = parts[0][...].astype(jnp.float32)
    for part in parts[1:]:
        unit = unit + part[...].astype(jnp.float32)
    own_ref[...] = unit
    low = unit.astype(jnp.bfloat16)
    send_ref[:, :D] = low[8:, :D]
    for b in range(4):
        send_ref[2 * b : 2 * b + 2, TAILS] = low[4 * b + 2 : 4 * b + 4, TAILS]
    lane = iota((8, LANES), 1)
    ends = jnp.concatenate([unit[2:4, SIDE], jnp.zeros((6, LANES), jnp.float32)], axis=0)
    send_ref[:, SIDE] = jnp.where(lane == 0, unit[8:, SIDE], ends).astype(jnp.bfloat16)


def last_kernel(
    mine, ids_ref, keep_ref, own_ref, got_ref, query_ref, sib_ref, near_ref, grad_ref, gate_ref, query_grad_ref
):
    query = query_ref[...] + sib_ref[...].astype(jnp.float32) + near_ref[...].astype(jnp.float32)
    query_grad_ref[...] = query.astype(jnp.bfloat16)
    ids, keep = ids_ref[...], keep_ref[...]
    tokens = ids.shape[1]
    expert = mine()
    diagonal = iota((tokens, tokens), 0) == iota((tokens, tokens), 1)
    own, got = own_ref[...], got_ref[...].astype(jnp.float32)
    grad = jnp.zeros((tokens, D), jnp.float32)
    gate = jnp.zeros((1, tokens), jnp.float32)
    for which, part, step in ((expert, own, 4), (1 - expert, got, 2)):
        slot = slots_of(ids, keep, which)
        column = jnp.sum(jnp.where(diagonal, slot, 0), axis=1, keepdims=True)
        ends = jnp.concatenate([part[step * b : step * b + 2, TAILS] for b in range(4)], axis=1)
        full = jnp.concatenate([part[:8, :D], ends, jnp.zeros((6, D), jnp.float32)], axis=0)
        grad = grad + mm(one_hot(iota((tokens, 16), 1) == column), full.astype(jnp.bfloat16))
        side = part[:, SIDE]
        gates = jnp.concatenate([side[:8, :1], side[:2, 1:2], jnp.zeros((6, 1), jnp.float32)], axis=0)
        gate = gate + jnp.sum(jnp.where(iota((16, tokens), 0) == slot, gates, 0.0), axis=0, keepdims=True)
    grad_ref[...] = grad.astype(jnp.bfloat16)
    gate_ref[...] = gate


def params(limit=4 * 2**20):
    return pltpu.CompilerParams(vmem_limit_bytes=limit)


def pack_tokens(query_ref, grad_ref, segments_ref, out_ref):
    tokens = query_ref.shape[0]
    out_ref[:tokens, :D] = (SCALE * query_ref[...].astype(jnp.float32)).astype(jnp.bfloat16)
    out_ref[tokens:, :D] = grad_ref[...]
    segments = segments_ref[...] + 1
    diagonal = iota((tokens, tokens), 0) == iota((tokens, tokens), 1)
    column = jnp.sum(jnp.where(diagonal, segments, 0), axis=1, keepdims=True)
    lane = iota((tokens, LANES), 1)
    digits = jnp.zeros((tokens, LANES), jnp.int32)
    for i in range(3):
        digits = digits + jnp.where(lane == i, (column >> (7 * i)) & 127, 0)
    out_ref[:tokens, D:] = digits.astype(jnp.float32).astype(jnp.bfloat16)
    out_ref[tokens:, D:] = jnp.zeros((tokens, LANES), jnp.bfloat16)


def segment_column(token_ref, tokens):
    digits = token_ref[:tokens, D:].astype(jnp.float32)
    lane = iota((tokens, LANES), 1)
    weight = jnp.zeros((tokens, LANES), jnp.float32)
    for i in range(3):
        weight = weight + jnp.where(lane == i, float(128**i), 0.0)
    return jnp.sum(weight * digits, axis=1, keepdims=True).astype(jnp.int32)


def head_scores(token_refs, kv, head, tokens):
    lanes = pl.ds(head * HEAD_DIM, HEAD_DIM)
    queries = jnp.concatenate([r[:tokens, lanes] for r in token_refs], axis=0)
    grads = jnp.concatenate([r[tokens : 2 * tokens, lanes] for r in token_refs], axis=0)
    both = mm(jnp.concatenate([queries, grads], axis=0), kv, ((1,), (1,)))
    count = queries.shape[0]
    return queries, grads, both[:count], pltpu.roll(both[count:], both.shape[1] - 1, 1)


def allowed_pairs(token_refs, rows_ref, tokens):
    column = jnp.concatenate([segment_column(r, tokens) for r in token_refs], axis=0)
    rows = rows_ref[...] + 1
    count = rows.shape[1]
    diagonal = iota((count, count), 0) == iota((count, count), 1)
    as_column = jnp.sum(jnp.where(diagonal, rows, 0), axis=1, keepdims=True)
    even = iota((count, 2 * count), 1) == 2 * iota((count, 2 * count), 0)
    spread = jnp.sum(jnp.where(even, as_column, 0), axis=0, keepdims=True)
    return jnp.where(spread > 0, spread, -1) == column


def load_head(kv_ref, head):
    rows = kv_ref.shape[0]
    return kv_ref[:, :, pl.ds(head * HEAD_DIM, HEAD_DIM)].reshape(2 * rows, HEAD_DIM)


def stats_kernel(own_ref, sib_ref, near_ref, rows_ref, kv_ref, stats_ref):
    token_refs = (own_ref, sib_ref, near_ref)
    tokens = own_ref.shape[0] // 2
    allowed = allowed_pairs(token_refs, rows_ref, tokens)
    valid = jnp.where(allowed, 1.0, 0.0)
    lane = iota((3 * tokens, LANES), 1)
    stats = jnp.zeros((3 * tokens, LANES), jnp.float32)
    for first in range(0, HEADS, GROUP):
        products = [
            head_scores(token_refs, load_head(kv_ref, first + i), first + i, tokens) for i in range(GROUP)
        ]
        for head, (_, _, scores, prob_grad) in enumerate(products, first):
            scores = jnp.where(allowed, scores, NONE)
            peak = jnp.max(scores, axis=1, keepdims=True)
            weight = jnp.exp(scores - peak) * valid
            mass = jnp.sum(weight, axis=1, keepdims=True)
            delta = jnp.sum(weight * prob_grad, axis=1, keepdims=True)
            stats = jnp.where(lane == head, peak, stats)
            stats = jnp.where(lane == HEADS + head, mass, stats)
            stats = jnp.where(lane == 2 * HEADS + head, delta, stats)
    stats_ref[...] = stats


def merged(parts):
    peaks = [jnp.where(p[:, HEADS : 2 * HEADS] > 0, p[:, :HEADS], NONE) for p in parts]
    peak = functools.reduce(jnp.maximum, peaks)
    scale = [jnp.exp(p - peak) for p in peaks]
    mass = sum(s * p[:, HEADS : 2 * HEADS] for s, p in zip(scale, parts))
    delta = sum(s * p[:, 2 * HEADS : 3 * HEADS] for s, p in zip(scale, parts))
    some = mass > 0
    mass = jnp.where(some, mass, 1.0)
    return jnp.where(some, peak + jnp.log(mass), 0.0), jnp.where(some, delta / mass, 0.0)


def grads_kernel(
    own_ref, sib_ref, near_ref, rows_ref, kv_ref, st_ref, st_sib_ref, met_ref, sib_met_ref,
    query_ref, to_sib_ref, to_near_ref, kv_grad_ref,
):
    token_refs = (own_ref, sib_ref, near_ref)
    tokens = own_ref.shape[0] // 2
    allowed = allowed_pairs(token_refs, rows_ref, tokens)
    a, b, c = slice(0, tokens), slice(tokens, 2 * tokens), slice(2 * tokens, 3 * tokens)
    far_b = slice(4 * tokens, 5 * tokens)
    totals = [
        merged((st_ref[a], st_sib_ref[b], met_ref[c])),
        merged((st_ref[b], st_sib_ref[a], sib_met_ref[c])),
        merged((st_ref[c], met_ref[a], met_ref[far_b])),
    ]
    total, delta = (jnp.concatenate([t[i] for t in totals], axis=0) for i in range(2))
    for first in range(0, HEADS, GROUP):
        kvs = [load_head(kv_ref, first + i) for i in range(GROUP)]
        products = [head_scores(token_refs, kv, first + i, tokens) for i, kv in enumerate(kvs)]
        lows = []
        for head, (_, _, scores, prob_grad) in enumerate(products, first):
            at = slice(head, head + 1)
            probs = jnp.exp(jnp.where(allowed, scores - total[:, at], NONE))
            score_grad = probs * (prob_grad - delta[:, at])
            moved = pltpu.roll(probs, 1, 1)
            lows.append((score_grad.astype(jnp.bfloat16), moved.astype(jnp.bfloat16)))
        for head, kv, (queries, grads, _, _), (score_low, probs_low) in zip(
            range(first, first + GROUP), kvs, products, lows
        ):
            lanes = pl.ds(head * HEAD_DIM, HEAD_DIM)
            query = SCALE * mm(score_low, kv)
            query_ref[:, lanes] = query[a]
            to_sib_ref[:, lanes] = query[b].astype(jnp.bfloat16)
            to_near_ref[:, lanes] = query[c].astype(jnp.bfloat16)
            both = jnp.concatenate([score_low, probs_low], axis=0)
            grad = mm(both, jnp.concatenate([queries, grads], axis=0), ((0,), (0,)))
            kv_grad_ref[:, :, lanes] = grad.astype(jnp.bfloat16).reshape(kv_grad_ref.shape[0], 2, HEAD_DIM)


def core(block):
    return lax.ppermute(block, "seq", [(i, i ^ 1) for i in range(lax.axis_size("seq"))])


def cross(block):
    crossing = [(i, i + 1) for i in range(1, lax.axis_size("seq") - 1, 2)]
    return lax.ppermute(block, "seq", crossing + [(j, i) for i, j in crossing])


def attention_stats(held):
    tokens = held[0].shape[0] // 2
    return pl.pallas_call(
        stats_kernel,
        out_shape=jax.ShapeDtypeStruct((3 * tokens, LANES), jnp.float32),
        compiler_params=params(12 * 2**20),
        cost_estimate=pl.CostEstimate(flops=10**9, bytes_accessed=16 * 10**6, transcendentals=0),
    )(*held)


def attention_grads(held, stats):
    tokens = held[0].shape[0] // 2
    low = jax.ShapeDtypeStruct((tokens, D), jnp.bfloat16)
    return pl.pallas_call(
        grads_kernel,
        out_shape=(
            jax.ShapeDtypeStruct((tokens, D), jnp.float32),
            low,
            low,
            jax.ShapeDtypeStruct(held[-1].shape, jnp.bfloat16),
        ),
        compiler_params=params(12 * 2**20),
        cost_estimate=pl.CostEstimate(flops=10**9, bytes_accessed=32 * 10**6, transcendentals=0),
    )(*held, *stats)


def after(value, *others):
    return lax.optimization_barrier((value, *others))[0]


def far(value):
    return pltpu.with_memory_space_constraint(value, pltpu.HBM)


def fetch_kernel(count, *refs):
    arrived = refs[2 * count]
    copies = [
        pltpu.make_async_copy(refs[i], refs[count + i], arrived.at[i]) for i in range(count)
    ]
    for copy in copies:
        copy.start()
    for copy in copies:
        copy.wait()


def fetch(*arrays):
    return pl.pallas_call(
        functools.partial(fetch_kernel, len(arrays)),
        in_specs=[pl.BlockSpec(memory_space=pltpu.HBM)] * len(arrays),
        out_specs=[pl.BlockSpec(memory_space=pltpu.VMEM)] * len(arrays),
        out_shape=[jax.ShapeDtypeStruct(a.shape, a.dtype) for a in arrays],
        scratch_shapes=[pltpu.SemaphoreType.DMA((len(arrays),))],
        compiler_params=params(24 * 2**20),
        cost_estimate=pl.CostEstimate(
            flops=0, bytes_accessed=sum(a.size * 2 for a in arrays), transcendentals=0
        ),
    )(*map(far, arrays))


def local(
    dec_query,
    ctx_grad,
    dec_segments,
    enc_kv,
    enc_segments,
    moe_input,
    moe_grad,
    gate_prob,
    expert_ids,
    keep_mask,
    w_input,
    w_output,
):
    devices = lax.axis_size("seq")
    shards = devices // EXPERTS
    tokens = moe_input.shape[0]
    width = w_input.shape[1]
    square = shards == 8

    def mine():
        return lax.axis_index("seq") // shards

    def flip(block, bits):
        return lax.ppermute(block, "seq", [(i, i ^ bits) for i in range(devices)])

    ids, keep = expert_ids.reshape(1, tokens), keep_mask.reshape(1, tokens)
    block_type = jax.ShapeDtypeStruct((16, WIDE), jnp.bfloat16)
    sent_type = jax.ShapeDtypeStruct((16, WIDE), jnp.bfloat16)
    own, other, packed = pl.pallas_call(
        functools.partial(pack_kernel, mine),
        out_shape=(sent_type, sent_type, jax.ShapeDtypeStruct((2 * tokens, D + LANES), jnp.bfloat16)),
        compiler_params=params(8 * 2**20),
    )(
        *map(far, (ids, keep, gate_prob.reshape(1, tokens), moe_input, moe_grad)),
        *map(far, (dec_query, ctx_grad, dec_segments.reshape(1, tokens))),
    )
    across = (devices - 1) & ~3
    got = flip(other, across)
    near_w_input, near_kv = w_input, enc_kv
    if square:
        near_w_input, near_kv = fetch(w_input, enc_kv)
    held = (packed, core(packed), cross(packed), far(enc_segments.reshape(1, -1)), near_kv)
    stats = attention_stats(held)
    stats_sib = core(stats)
    met = cross(jnp.concatenate([stats, stats_sib]))
    all_stats = (stats, stats_sib, met, core(met))

    pair = jnp.concatenate([own, got])
    if square:
        pair = after(pair, held[1], held[2], near_kv)
        near = [pair, flip(pair, 2), flip(pair, 4), flip(pair, 6)]
        beside = flip(pair, 1)
        near[1:3] = after(near[1:3], stats_sib)
        near[3], all_stats = lax.optimization_barrier((near[3], all_stats))
        blocks = [b[None] for b in near + [beside] + [flip(b, 1) for b in near[1:]]]
    else:
        halves = [list(range(e * shards, (e + 1) * shards)) for e in range(EXPERTS)]
        blocks = [lax.all_gather(pair[None], "seq", axis_index_groups=halves, tiled=True)]
    places, at = [], 0
    for b in blocks:
        places.append(at)
        at += b.shape[0]
    sources = 2 * at
    rows = sources * CAP
    keep_units = shards // 2
    slots = jax.ShapeDtypeStruct((rows, D), jnp.bfloat16)
    hidden_type = jax.ShapeDtypeStruct((rows, width), jnp.bfloat16)
    units_type = jax.ShapeDtypeStruct((keep_units, 16, WIDE), jnp.bfloat16)
    x, g, hidden, scaled, keep_half, send_half = pl.pallas_call(
        functools.partial(main_kernel, places),
        out_shape=[slots, slots, hidden_type, hidden_type, units_type, units_type],
        in_specs=[pl.BlockSpec(memory_space=pltpu.VMEM)] * len(places)
        + [pl.BlockSpec(memory_space=pltpu.VMEM), pl.BlockSpec(memory_space=pltpu.HBM)],
        scratch_shapes=[
            pltpu.VMEM((4 * sources, D), jnp.bfloat16),
            pltpu.VMEM((rows, LANES), jnp.float32),
            pltpu.VMEM((rows, width), jnp.float32),
            pltpu.VMEM((width, D), jnp.bfloat16),
            pltpu.SemaphoreType.DMA,
        ],
        compiler_params=params(MAIN_LIMIT if square else 62 * 2**20),
        cost_estimate=pl.CostEstimate(flops=6 * rows * D * width, bytes_accessed=4 * D * width, transcendentals=0),
    )(*blocks, near_w_input, far(w_output))

    unit_wide = jax.ShapeDtypeStruct((16, WIDE), jnp.float32)
    tail_type = jax.ShapeDtypeStruct((8, WIDE), jnp.bfloat16)
    if square:
        swapped = flip(send_half, 1)
        summed = pl.pallas_call(
            sum_pairs_kernel,
            out_shape=[unit_wide] + [block_type] * 3,
            compiler_params=params(),
        )(keep_half, swapped)
        parts = [summed[0], flip(summed[1], 2), flip(summed[2], 4), flip(summed[3], 6)]
        all_stats = after(all_stats, summed[0])
    else:
        units = jnp.concatenate([keep_half, send_half]).astype(jnp.float32)
        parts = [
            lax.psum_scatter(units, "seq", axis_index_groups=halves, tiled=True).reshape(16, WIDE)
        ]
    query, to_sib, to_near, kv_grad = attention_grads(held, all_stats)
    parts[0] = after(parts[0], query)
    own_unit, send_unit = pl.pallas_call(
        sum_unit_kernel, out_shape=(unit_wide, tail_type), compiler_params=params()
    )(*parts)
    returned = flip(send_unit, across)
    to_sib, to_near = after((to_sib, to_near), own_unit)
    from_sib, from_near = core(to_sib), cross(to_near)

    x, hidden, scaled, g = after((x, hidden, scaled, g), own_unit)
    pieces = max(1, min(4, width // 128))
    once = pl.Buffered(1)
    w_input_grad, w_output_grad = pl.pallas_call(
        weights_kernel,
        grid=(pieces,),
        in_specs=[
            pl.BlockSpec((rows, D // pieces), lambda i: (0, i)),
            pl.BlockSpec((rows, width), lambda i: (0, 0), pipeline_mode=once),
            pl.BlockSpec((rows, width // pieces), lambda i: (0, i)),
            pl.BlockSpec((rows, D), lambda i: (0, 0), pipeline_mode=once),
        ],
        out_specs=[
            pl.BlockSpec((D // pieces, width), lambda i: (i, 0)),
            pl.BlockSpec((width // pieces, D), lambda i: (i, 0)),
        ],
        out_shape=[
            jax.ShapeDtypeStruct((D, width), jnp.bfloat16),
            jax.ShapeDtypeStruct((width, D), jnp.bfloat16),
        ],
        compiler_params=params(24 * 2**20),
        cost_estimate=pl.CostEstimate(flops=4 * rows * D * width, bytes_accessed=4 * D * width, transcendentals=0),
    )(x, hidden, scaled, g)

    moe_input_grad, gate_grad, query_grad = pl.pallas_call(
        functools.partial(last_kernel, mine),
        out_shape=(
            jax.ShapeDtypeStruct((tokens, D), jnp.bfloat16),
            jax.ShapeDtypeStruct((1, tokens), jnp.float32),
            jax.ShapeDtypeStruct((tokens, D), jnp.bfloat16),
        ),
        compiler_params=params(),
    )(ids, keep, own_unit, returned, query, from_sib, from_near)
    return (
        query_grad,
        kv_grad,
        moe_input_grad,
        gate_grad.reshape(tokens),
        w_input_grad,
        w_output_grad,
    )


def solution(mesh):
    return jax.shard_map(
        local,
        mesh=mesh,
        in_specs=(
            P(("groups", "seq"), None),
            P(("groups", "seq"), None),
            P(("groups", "seq")),
            P(("groups", "seq"), None, None),
            P(("groups", "seq")),
            P(("groups", "seq"), None),
            P(("groups", "seq"), None),
            P(("groups", "seq")),
            P(("groups", "seq")),
            P(("groups", "seq")),
            P(None, "seq"),
            P("seq", None),
        ),
        out_specs=(
            P(("groups", "seq"), None),
            P(("groups", "seq"), None, None),
            P(("groups", "seq"), None),
            P(("groups", "seq")),
            P("groups", "seq"),
            P("seq", "groups"),
        ),
        check_vma=False,
    )
```

```python
import functools

import jax
import jax.numpy as jnp
from jax import lax
from jax.experimental import pallas as pl
from jax.experimental.pallas import tpu as pltpu
from jax.sharding import PartitionSpec as P

D = 4096
HEADS = 32
HEAD_DIM = 128
EXPERTS = 2
CAP = 10
SCALE = 0.125
NONE = -1e30
LANES = 128
FOLD = D // 4
WIDE = D + FOLD + LANES
TAILS = slice(D, D + FOLD)
SIDE = slice(D + FOLD, WIDE)
GROUP = 4
MAIN_LIMIT = 24 * 2**20


def iota(shape, dim):
    return lax.broadcasted_iota(jnp.int32, shape, dim)


def one_hot(mask):
    return jnp.where(mask, 1.0, 0.0).astype(jnp.bfloat16)


def mm(a, b, dims=((1,), (0,))):
    return lax.dot_general(a, b, (dims, ((), ())), preferred_element_type=jnp.float32)


def slots_of(ids, keep, expert):
    tokens = ids.shape[1]
    row, col = iota((tokens, tokens), 0), iota((tokens, tokens), 1)
    chosen = (ids == expert) & (keep == 1)
    chosen_f = jnp.where(chosen, 1.0, 0.0)
    as_column = jnp.sum(jnp.where(row == col, chosen_f, 0.0), axis=1, keepdims=True)
    earlier = jnp.sum(jnp.where(row < col, as_column, 0.0), axis=0, keepdims=True)
    slot = earlier.astype(jnp.int32)
    return jnp.where(chosen & (slot < CAP), slot, -1)


def pack_kernel(
    mine, ids_ref, keep_ref, gate_ref, input_ref, grad_ref, query_ref, ctx_ref, segments_ref,
    own_ref, other_ref, tokens_ref,
):
    pack_tokens(query_ref, ctx_ref, segments_ref, tokens_ref)
    ids, keep = ids_ref[...], keep_ref[...]
    tokens = ids.shape[1]
    gate = gate_ref[...].astype(jnp.float32)
    moe_input, moe_grad = input_ref[...], grad_ref[...]
    expert = mine()
    row = iota((24, tokens), 0)
    input_slot = jnp.where(row < 8, row, jnp.where((row == 16) | (row == 17), row - 8, -2))
    grad_slot = jnp.where(
        (row >= 8) & (row < 16), row - 8, jnp.where((row == 18) | (row == 19), row - 10, -2)
    )
    gate_slot = jnp.where(row < CAP, row, -2)
    for which, out_ref in ((expert, own_ref), (1 - expert, other_ref)):
        slot = slots_of(ids, keep, which)
        block = mm(one_hot(input_slot == slot), moe_input) + mm(one_hot(grad_slot == slot), moe_grad)
        block = block.astype(jnp.bfloat16)
        out_ref[:, :D] = block[:16]
        for b in range(4):
            out_ref[4 * b : 4 * b + 4, TAILS] = block[16:20, b * FOLD : (b + 1) * FOLD]
        gates = jnp.sum(jnp.where(gate_slot == slot, gate, 0.0), axis=1, keepdims=True)
        out_ref[:, SIDE] = jnp.broadcast_to(gates[:16], (16, LANES)).astype(jnp.bfloat16)


def main_kernel(places, *refs):
    blocks, refs = refs[: len(places)], refs[len(places) :]
    w_in_ref, w_out_far, x_out, g_out, hidden_ref, scaled_ref, keep_ref, send_ref = refs[:8]
    tails, gate_ref, pre_ref, w_out_ref, arrived = refs[8:]
    fetched = pltpu.make_async_copy(w_out_far, w_out_ref, arrived)
    fetched.start()
    units = sum(r.shape[0] for r in blocks)
    heads, rows = 16 * units, 20 * units
    width = w_in_ref.shape[1]
    chunk = min(width, 256)
    for block, place in zip(blocks, places):
        for i in range(block.shape[0]):
            at = place + i
            pair = block[i]
            both = jnp.concatenate([pair[:8], pair[16:24]], axis=0)
            x_out[pl.ds(16 * at, 16), :] = both[:, :D]
            gate_ref[pl.ds(16 * at, 16), :] = both[:, SIDE].astype(jnp.float32)
            g_out[pl.ds(16 * at, 16), :] = jnp.concatenate([pair[8:16, :D], pair[24:32, :D]], axis=0)
            gate_ref[pl.ds(heads + 4 * at, 4), :] = jnp.concatenate(
                [pair[8:10, SIDE], pair[24:26, SIDE]], axis=0
            ).astype(jnp.float32)
            for b in range(4):
                tails[pl.ds(8 * at, 8), pl.ds(b * FOLD, FOLD)] = jnp.concatenate(
                    [pair[4 * b : 4 * b + 4, TAILS], pair[16 + 4 * b : 20 + 4 * b, TAILS]], axis=0
                )
    row, col = iota((4 * units, 8 * units), 0), iota((4 * units, 8 * units), 1)
    pick = 4 * (row // 2) + row % 2
    tail = tails[...]
    x_out[pl.ds(heads, 4 * units), :] = mm(one_hot(col == pick), tail).astype(jnp.bfloat16)
    g_out[pl.ds(heads, 4 * units), :] = mm(one_hot(col == pick + 2), tail).astype(jnp.bfloat16)
    gate = gate_ref[:, :1]

    for start in range(0, width, chunk):
        at = pl.ds(start, chunk)
        pre_ref[:, at] = mm(x_out[...], w_in_ref[:, at])
    fetched.wait()
    gate_part = jnp.zeros((rows, 1), jnp.float32)
    for start in range(0, width, chunk):
        at = pl.ds(start, chunk)
        pre = pre_ref[:, at]
        back = mm(g_out[...], w_out_ref[at, :], ((1,), (1,)))
        active = jnp.maximum(pre, 0.0)
        hidden_ref[:, at] = (gate * back * jnp.where(pre > 0, 1.0, 0.0)).astype(jnp.bfloat16)
        scaled_ref[:, at] = (gate * active).astype(jnp.bfloat16)
        gate_part += jnp.sum(active * back, axis=1, keepdims=True)

    halves = [(keep_ref, u) for u in range(keep_ref.shape[0])] + [(send_ref, u) for u in range(send_ref.shape[0])]
    hidden = hidden_ref[...]
    for b in range(4):
        lanes = pl.ds(b * FOLD, FOLD)
        part = mm(hidden, w_in_ref[lanes, :], ((1,), (1,))).astype(jnp.bfloat16)
        for u, (half, index) in enumerate(halves):
            half[index, :, lanes] = part[16 * u : 16 * u + 16]
            half[index, 4 * b : 4 * b + 4, TAILS] = part[heads + 4 * u : heads + 4 * u + 4]
    lane = iota((16, LANES), 1)
    for u, (half, index) in enumerate(halves):
        ends = gate_part[heads + 4 * u : heads + 4 * u + 4]
        ends = jnp.concatenate([ends, jnp.zeros((12, 1), jnp.float32)], axis=0)
        side = jnp.where(lane == 0, gate_part[16 * u : 16 * u + 16], jnp.where(lane == 1, ends, 0.0))
        half[index, :, SIDE] = side.astype(jnp.bfloat16)


def weights_kernel(x_ref, hidden_ref, scaled_ref, g_ref, w_in_ref, w_out_ref):
    w_in_ref[...] = mm(x_ref[...], hidden_ref[...], ((0,), (0,))).astype(jnp.bfloat16)
    w_out_ref[...] = mm(scaled_ref[...], g_ref[...], ((0,), (0,))).astype(jnp.bfloat16)


def sum_pairs_kernel(keep_ref, got_ref, own_ref, *out_refs):
    own_ref[...] = keep_ref[0].astype(jnp.float32) + got_ref[0].astype(jnp.float32)
    for i, out_ref in enumerate(out_refs):
        out_ref[...] = (
            keep_ref[i + 1].astype(jnp.float32) + got_ref[i + 1].astype(jnp.float32)
        ).astype(jnp.bfloat16)


def sum_unit_kernel(*refs):
    parts, (own_ref, send_ref) = refs[:-2], refs[-2:]
    unit = parts[0][...].astype(jnp.float32)
    for part in parts[1:]:
        unit = unit + part[...].astype(jnp.float32)
    own_ref[...] = unit
    low = unit.astype(jnp.bfloat16)
    send_ref[:, :D] = low[8:, :D]
    for b in range(4):
        send_ref[2 * b : 2 * b + 2, TAILS] = low[4 * b + 2 : 4 * b + 4, TAILS]
    lane = iota((8, LANES), 1)
    ends = jnp.concatenate([unit[2:4, SIDE], jnp.zeros((6, LANES), jnp.float32)], axis=0)
    send_ref[:, SIDE] = jnp.where(lane == 0, unit[8:, SIDE], ends).astype(jnp.bfloat16)


def last_kernel(
    mine, ids_ref, keep_ref, own_ref, got_ref, query_ref, sib_ref, near_ref, grad_ref, gate_ref, query_grad_ref
):
    query = query_ref[...] + sib_ref[...].astype(jnp.float32) + near_ref[...].astype(jnp.float32)
    query_grad_ref[...] = query.astype(jnp.bfloat16)
    ids, keep = ids_ref[...], keep_ref[...]
    tokens = ids.shape[1]
    expert = mine()
    diagonal = iota((tokens, tokens), 0) == iota((tokens, tokens), 1)
    own, got = own_ref[...], got_ref[...].astype(jnp.float32)
    grad = jnp.zeros((tokens, D), jnp.float32)
    gate = jnp.zeros((1, tokens), jnp.float32)
    for which, part, step in ((expert, own, 4), (1 - expert, got, 2)):
        slot = slots_of(ids, keep, which)
        column = jnp.sum(jnp.where(diagonal, slot, 0), axis=1, keepdims=True)
        ends = jnp.concatenate([part[step * b : step * b + 2, TAILS] for b in range(4)], axis=1)
        full = jnp.concatenate([part[:8, :D], ends, jnp.zeros((6, D), jnp.float32)], axis=0)
        grad = grad + mm(one_hot(iota((tokens, 16), 1) == column), full.astype(jnp.bfloat16))
        side = part[:, SIDE]
        gates = jnp.concatenate([side[:8, :1], side[:2, 1:2], jnp.zeros((6, 1), jnp.float32)], axis=0)
        gate = gate + jnp.sum(jnp.where(iota((16, tokens), 0) == slot, gates, 0.0), axis=0, keepdims=True)
    grad_ref[...] = grad.astype(jnp.bfloat16)
    gate_ref[...] = gate


def params(limit=4 * 2**20):
    return pltpu.CompilerParams(vmem_limit_bytes=limit)


def pack_tokens(query_ref, grad_ref, segments_ref, out_ref):
    tokens = query_ref.shape[0]
    out_ref[:tokens, :D] = (SCALE * query_ref[...].astype(jnp.float32)).astype(jnp.bfloat16)
    out_ref[tokens:, :D] = grad_ref[...]
    segments = segments_ref[...] + 1
    diagonal = iota((tokens, tokens), 0) == iota((tokens, tokens), 1)
    column = jnp.sum(jnp.where(diagonal, segments, 0), axis=1, keepdims=True)
    lane = iota((tokens, LANES), 1)
    digits = jnp.zeros((tokens, LANES), jnp.int32)
    for i in range(3):
        digits = digits + jnp.where(lane == i, (column >> (7 * i)) & 127, 0)
    out_ref[:tokens, D:] = digits.astype(jnp.float32).astype(jnp.bfloat16)
    out_ref[tokens:, D:] = jnp.zeros((tokens, LANES), jnp.bfloat16)


def segment_column(token_ref, tokens):
    digits = token_ref[:tokens, D:].astype(jnp.float32)
    lane = iota((tokens, LANES), 1)
    weight = jnp.zeros((tokens, LANES), jnp.float32)
    for i in range(3):
        weight = weight + jnp.where(lane == i, float(128**i), 0.0)
    return jnp.sum(weight * digits, axis=1, keepdims=True).astype(jnp.int32)


def head_scores(token_refs, kv, head, tokens):
    lanes = pl.ds(head * HEAD_DIM, HEAD_DIM)
    queries = jnp.concatenate([r[:tokens, lanes] for r in token_refs], axis=0)
    grads = jnp.concatenate([r[tokens : 2 * tokens, lanes] for r in token_refs], axis=0)
    both = mm(jnp.concatenate([queries, grads], axis=0), kv, ((1,), (1,)))
    count = queries.shape[0]
    return queries, grads, both[:count], pltpu.roll(both[count:], both.shape[1] - 1, 1)


def allowed_pairs(token_refs, rows_ref, tokens):
    column = jnp.concatenate([segment_column(r, tokens) for r in token_refs], axis=0)
    rows = rows_ref[...] + 1
    count = rows.shape[1]
    diagonal = iota((count, count), 0) == iota((count, count), 1)
    as_column = jnp.sum(jnp.where(diagonal, rows, 0), axis=1, keepdims=True)
    even = iota((count, 2 * count), 1) == 2 * iota((count, 2 * count), 0)
    spread = jnp.sum(jnp.where(even, as_column, 0), axis=0, keepdims=True)
    return jnp.where(spread > 0, spread, -1) == column


def load_head(kv_ref, head):
    rows = kv_ref.shape[0]
    return kv_ref[:, :, pl.ds(head * HEAD_DIM, HEAD_DIM)].reshape(2 * rows, HEAD_DIM)


def stats_kernel(own_ref, sib_ref, near_ref, rows_ref, kv_ref, stats_ref):
    token_refs = (own_ref, sib_ref, near_ref)
    tokens = own_ref.shape[0] // 2
    allowed = allowed_pairs(token_refs, rows_ref, tokens)
    valid = jnp.where(allowed, 1.0, 0.0)
    lane = iota((3 * tokens, LANES), 1)
    stats = jnp.zeros((3 * tokens, LANES), jnp.float32)
    for first in range(0, HEADS, GROUP):
        products = [
            head_scores(token_refs, load_head(kv_ref, first + i), first + i, tokens) for i in range(GROUP)
        ]
        for head, (_, _, scores, prob_grad) in enumerate(products, first):
            scores = jnp.where(allowed, scores, NONE)
            peak = jnp.max(scores, axis=1, keepdims=True)
            weight = jnp.exp(scores - peak) * valid
            mass = jnp.sum(weight, axis=1, keepdims=True)
            delta = jnp.sum(weight * prob_grad, axis=1, keepdims=True)
            stats = jnp.where(lane == head, peak, stats)
            stats = jnp.where(lane == HEADS + head, mass, stats)
            stats = jnp.where(lane == 2 * HEADS + head, delta, stats)
    stats_ref[...] = stats


def merged(parts):
    peaks = [jnp.where(p[:, HEADS : 2 * HEADS] > 0, p[:, :HEADS], NONE) for p in parts]
    peak = functools.reduce(jnp.maximum, peaks)
    scale = [jnp.exp(p - peak) for p in peaks]
    mass = sum(s * p[:, HEADS : 2 * HEADS] for s, p in zip(scale, parts))
    delta = sum(s * p[:, 2 * HEADS : 3 * HEADS] for s, p in zip(scale, parts))
    some = mass > 0
    mass = jnp.where(some, mass, 1.0)
    return jnp.where(some, peak + jnp.log(mass), 0.0), jnp.where(some, delta / mass, 0.0)


def grads_kernel(
    own_ref, sib_ref, near_ref, rows_ref, kv_ref, st_ref, st_sib_ref, met_ref, sib_met_ref,
    query_ref, to_sib_ref, to_near_ref, kv_grad_ref,
):
    token_refs = (own_ref, sib_ref, near_ref)
    tokens = own_ref.shape[0] // 2
    allowed = allowed_pairs(token_refs, rows_ref, tokens)
    a, b, c = slice(0, tokens), slice(tokens, 2 * tokens), slice(2 * tokens, 3 * tokens)
    far_b = slice(4 * tokens, 5 * tokens)
    totals = [
        merged((st_ref[a], st_sib_ref[b], met_ref[c])),
        merged((st_ref[b], st_sib_ref[a], sib_met_ref[c])),
        merged((st_ref[c], met_ref[a], met_ref[far_b])),
    ]
    total, delta = (jnp.concatenate([t[i] for t in totals], axis=0) for i in range(2))
    for first in range(0, HEADS, GROUP):
        kvs = [load_head(kv_ref, first + i) for i in range(GROUP)]
        products = [head_scores(token_refs, kv, first + i, tokens) for i, kv in enumerate(kvs)]
        lows = []
        for head, (_, _, scores, prob_grad) in enumerate(products, first):
            at = slice(head, head + 1)
            probs = jnp.exp(jnp.where(allowed, scores - total[:, at], NONE))
            score_grad = probs * (prob_grad - delta[:, at])
            moved = pltpu.roll(probs, 1, 1)
            lows.append((score_grad.astype(jnp.bfloat16), moved.astype(jnp.bfloat16)))
        for head, kv, (queries, grads, _, _), (score_low, probs_low) in zip(
            range(first, first + GROUP), kvs, products, lows
        ):
            lanes = pl.ds(head * HEAD_DIM, HEAD_DIM)
            query = SCALE * mm(score_low, kv)
            query_ref[:, lanes] = query[a]
            to_sib_ref[:, lanes] = query[b].astype(jnp.bfloat16)
            to_near_ref[:, lanes] = query[c].astype(jnp.bfloat16)
            both = jnp.concatenate([score_low, probs_low], axis=0)
            grad = mm(both, jnp.concatenate([queries, grads], axis=0), ((0,), (0,)))
            kv_grad_ref[:, :, lanes] = grad.astype(jnp.bfloat16).reshape(kv_grad_ref.shape[0], 2, HEAD_DIM)


def core(block):
    return lax.ppermute(block, "seq", [(i, i ^ 1) for i in range(lax.axis_size("seq"))])


def cross(block):
    crossing = [(i, i + 1) for i in range(1, lax.axis_size("seq") - 1, 2)]
    return lax.ppermute(block, "seq", crossing + [(j, i) for i, j in crossing])


def attention_stats(held):
    tokens = held[0].shape[0] // 2
    return pl.pallas_call(
        stats_kernel,
        out_shape=jax.ShapeDtypeStruct((3 * tokens, LANES), jnp.float32),
        compiler_params=params(12 * 2**20),
        cost_estimate=pl.CostEstimate(flops=10**9, bytes_accessed=16 * 10**6, transcendentals=0),
    )(*held)


def attention_grads(held, stats):
    tokens = held[0].shape[0] // 2
    low = jax.ShapeDtypeStruct((tokens, D), jnp.bfloat16)
    return pl.pallas_call(
        grads_kernel,
        out_shape=(
            jax.ShapeDtypeStruct((tokens, D), jnp.float32),
            low,
            low,
            jax.ShapeDtypeStruct(held[-1].shape, jnp.bfloat16),
        ),
        compiler_params=params(12 * 2**20),
        cost_estimate=pl.CostEstimate(flops=10**9, bytes_accessed=32 * 10**6, transcendentals=0),
    )(*held, *stats)


def after(value, *others):
    return lax.optimization_barrier((value, *others))[0]


def far(value):
    return pltpu.with_memory_space_constraint(value, pltpu.HBM)


def fetch_kernel(count, *refs):
    arrived = refs[2 * count]
    copies = [
        pltpu.make_async_copy(refs[i], refs[count + i], arrived.at[i]) for i in range(count)
    ]
    for copy in copies:
        copy.start()
    for copy in copies:
        copy.wait()


def fetch(*arrays):
    return pl.pallas_call(
        functools.partial(fetch_kernel, len(arrays)),
        in_specs=[pl.BlockSpec(memory_space=pltpu.HBM)] * len(arrays),
        out_specs=[pl.BlockSpec(memory_space=pltpu.VMEM)] * len(arrays),
        out_shape=[jax.ShapeDtypeStruct(a.shape, a.dtype) for a in arrays],
        scratch_shapes=[pltpu.SemaphoreType.DMA((len(arrays),))],
        compiler_params=params(24 * 2**20),
        cost_estimate=pl.CostEstimate(
            flops=0, bytes_accessed=sum(a.size * 2 for a in arrays), transcendentals=0
        ),
    )(*map(far, arrays))


def local(
    dec_query,
    ctx_grad,
    dec_segments,
    enc_kv,
    enc_segments,
    moe_input,
    moe_grad,
    gate_prob,
    expert_ids,
    keep_mask,
    w_input,
    w_output,
):
    devices = lax.axis_size("seq")
    shards = devices // EXPERTS
    tokens = moe_input.shape[0]
    width = w_input.shape[1]
    square = shards == 8

    def mine():
        return lax.axis_index("seq") // shards

    def flip(block, bits):
        return lax.ppermute(block, "seq", [(i, i ^ bits) for i in range(devices)])

    ids, keep = expert_ids.reshape(1, tokens), keep_mask.reshape(1, tokens)
    block_type = jax.ShapeDtypeStruct((16, WIDE), jnp.bfloat16)
    sent_type = jax.ShapeDtypeStruct((16, WIDE), jnp.bfloat16)
    own, other, packed = pl.pallas_call(
        functools.partial(pack_kernel, mine),
        out_shape=(sent_type, sent_type, jax.ShapeDtypeStruct((2 * tokens, D + LANES), jnp.bfloat16)),
        compiler_params=params(8 * 2**20),
    )(
        *map(far, (ids, keep, gate_prob.reshape(1, tokens), moe_input, moe_grad)),
        *map(far, (dec_query, ctx_grad, dec_segments.reshape(1, tokens))),
    )
    across = (devices - 1) & ~3
    got = flip(other, across)
    near_w_input, near_kv = w_input, enc_kv
    if square:
        near_w_input, near_kv = fetch(w_input, enc_kv)
    held = (packed, core(packed), cross(packed), far(enc_segments.reshape(1, -1)), near_kv)
    stats = attention_stats(held)
    stats_sib = core(stats)
    met = cross(jnp.concatenate([stats, stats_sib]))
    all_stats = (stats, stats_sib, met, core(met))

    pair = jnp.concatenate([own, got])
    if square:
        pair = after(pair, held[1], held[2], near_kv)
        near = [pair, flip(pair, 2), flip(pair, 4), flip(pair, 6)]
        beside = flip(pair, 1)
        near[2:] = after(near[2:], stats_sib)
        near[1], met = lax.optimization_barrier((near[1], met))
        all_stats = (stats, stats_sib, met, core(met))
        beside, all_stats = lax.optimization_barrier((beside, all_stats))
        blocks = [b[None] for b in near + [beside] + [flip(b, 1) for b in near[1:]]]
    else:
        halves = [list(range(e * shards, (e + 1) * shards)) for e in range(EXPERTS)]
        blocks = [lax.all_gather(pair[None], "seq", axis_index_groups=halves, tiled=True)]
    places, at = [], 0
    for b in blocks:
        places.append(at)
        at += b.shape[0]
    sources = 2 * at
    rows = sources * CAP
    keep_units = shards // 2
    slots = jax.ShapeDtypeStruct((rows, D), jnp.bfloat16)
    hidden_type = jax.ShapeDtypeStruct((rows, width), jnp.bfloat16)
    units_type = jax.ShapeDtypeStruct((keep_units, 16, WIDE), jnp.bfloat16)
    x, g, hidden, scaled, keep_half, send_half = pl.pallas_call(
        functools.partial(main_kernel, places),
        out_shape=[slots, slots, hidden_type, hidden_type, units_type, units_type],
        in_specs=[pl.BlockSpec(memory_space=pltpu.VMEM)] * len(places)
        + [pl.BlockSpec(memory_space=pltpu.VMEM), pl.BlockSpec(memory_space=pltpu.HBM)],
        scratch_shapes=[
            pltpu.VMEM((4 * sources, D), jnp.bfloat16),
            pltpu.VMEM((rows, LANES), jnp.float32),
            pltpu.VMEM((rows, width), jnp.float32),
            pltpu.VMEM((width, D), jnp.bfloat16),
            pltpu.SemaphoreType.DMA,
        ],
        compiler_params=params(MAIN_LIMIT if square else 62 * 2**20),
        cost_estimate=pl.CostEstimate(flops=6 * rows * D * width, bytes_accessed=4 * D * width, transcendentals=0),
    )(*blocks, near_w_input, far(w_output))

    unit_wide = jax.ShapeDtypeStruct((16, WIDE), jnp.float32)
    tail_type = jax.ShapeDtypeStruct((8, WIDE), jnp.bfloat16)
    if square:
        swapped = flip(send_half, 1)
        summed = pl.pallas_call(
            sum_pairs_kernel,
            out_shape=[unit_wide] + [block_type] * 3,
            compiler_params=params(),
        )(keep_half, swapped)
        parts = [summed[0], flip(summed[1], 2), flip(summed[2], 4), flip(summed[3], 6)]
        all_stats = after(all_stats, summed[0])
    else:
        units = jnp.concatenate([keep_half, send_half]).astype(jnp.float32)
        parts = [
            lax.psum_scatter(units, "seq", axis_index_groups=halves, tiled=True).reshape(16, WIDE)
        ]
    query, to_sib, to_near, kv_grad = attention_grads(held, all_stats)
    parts[0] = after(parts[0], query)
    own_unit, send_unit = pl.pallas_call(
        sum_unit_kernel, out_shape=(unit_wide, tail_type), compiler_params=params()
    )(*parts)
    returned = flip(send_unit, across)
    to_sib, to_near = after((to_sib, to_near), own_unit)
    from_sib, from_near = core(to_sib), cross(to_near)

    x, hidden, scaled, g = after((x, hidden, scaled, g), own_unit)
    pieces = max(1, min(4, width // 128))
    once = pl.Buffered(1)
    w_input_grad, w_output_grad = pl.pallas_call(
        weights_kernel,
        grid=(pieces,),
        in_specs=[
            pl.BlockSpec((rows, D // pieces), lambda i: (0, i)),
            pl.BlockSpec((rows, width), lambda i: (0, 0), pipeline_mode=once),
            pl.BlockSpec((rows, width // pieces), lambda i: (0, i)),
            pl.BlockSpec((rows, D), lambda i: (0, 0), pipeline_mode=once),
        ],
        out_specs=[
            pl.BlockSpec((D // pieces, width), lambda i: (i, 0)),
            pl.BlockSpec((width // pieces, D), lambda i: (i, 0)),
        ],
        out_shape=[
            jax.ShapeDtypeStruct((D, width), jnp.bfloat16),
            jax.ShapeDtypeStruct((width, D), jnp.bfloat16),
        ],
        compiler_params=params(24 * 2**20),
        cost_estimate=pl.CostEstimate(flops=4 * rows * D * width, bytes_accessed=4 * D * width, transcendentals=0),
    )(x, hidden, scaled, g)

    moe_input_grad, gate_grad, query_grad = pl.pallas_call(
        functools.partial(last_kernel, mine),
        out_shape=(
            jax.ShapeDtypeStruct((tokens, D), jnp.bfloat16),
            jax.ShapeDtypeStruct((1, tokens), jnp.float32),
            jax.ShapeDtypeStruct((tokens, D), jnp.bfloat16),
        ),
        compiler_params=params(),
    )(ids, keep, own_unit, returned, query, from_sib, from_near)
    return (
        query_grad,
        kv_grad,
        moe_input_grad,
        gate_grad.reshape(tokens),
        w_input_grad,
        w_output_grad,
    )


def solution(mesh):
    return jax.shard_map(
        local,
        mesh=mesh,
        in_specs=(
            P(("groups", "seq"), None),
            P(("groups", "seq"), None),
            P(("groups", "seq")),
            P(("groups", "seq"), None, None),
            P(("groups", "seq")),
            P(("groups", "seq"), None),
            P(("groups", "seq"), None),
            P(("groups", "seq")),
            P(("groups", "seq")),
            P(("groups", "seq")),
            P(None, "seq"),
            P("seq", None),
        ),
        out_specs=(
            P(("groups", "seq"), None),
            P(("groups", "seq"), None, None),
            P(("groups", "seq"), None),
            P(("groups", "seq")),
            P("groups", "seq"),
            P("seq", "groups"),
        ),
        check_vma=False,
    )
```
